128 devices in a mesh: dp: 16 (over x, y), seq: 8 (over z, core).
Axes of the slice: x: 4, y: 4, z: 4, core: 2. Of those that a mesh axis runs over, the one named last changes fastest.
Arguments:
- tokens: bfloat16 [16, 512, 2048], P('dp', 'seq'), may hold values from -6 to 6
- memory: bfloat16 [16, 2048, 2048], P('dp', 'seq'), may hold values from -6 to 6
- mem_session: int32 [16, 2048], P('dp', 'seq'), may hold values from 0 to 3, never falling along the last dimension, each value on 1 to 1024 neighbouring positions
- dec_session: int32 [16, 512], P('dp', 'seq'), may hold values from 0 to 3, never falling along the last dimension, each value on 1 to 256 neighbouring positions
- event_bias: float32 [16, 2, 2048], P('dp', None, 'seq'), may hold values from -6 to 263
- expert_ids: int32 [16, 512, 2], P('dp', 'seq'), may hold values from 0 to 23, all different within a row; in each aligned block of 64 rows (0 to 63, 64 to 127, ..., all dimensions but the last counted through in order) at most 6 rows name the same one
- route_weights: float32 [16, 512, 2], P('dp', 'seq'), may hold values from 0.2 to 1
- norm_gain: float32 [2048], replicated, may hold values from 0.25 to 1.75
- w_query: bfloat16 [2048, 1024], P('seq'), may hold values from -0.125 to 0.125
- w_keyval: bfloat16 [2048, 512], P('seq'), may hold values from -0.125 to 0.125
- w_output: bfloat16 [1024, 2048], P('seq'), may hold values from -0.1875 to 0.1875
- w_gate: bfloat16 [24, 2048, 4096], P('seq', None, 'dp'), may hold values from -0.125 to 0.125
- w_up: bfloat16 [24, 2048, 4096], P('seq', None, 'dp'), may hold values from -0.125 to 0.125
- w_down: bfloat16 [24, 4096, 2048], P('seq', 'dp'), may hold values from -0.09375 to 0.09375
- cotangent: bfloat16 [16, 512, 2048], P('dp', 'seq'), may hold values from -6 to 6
Outputs:
- block_out: bfloat16 [16, 512, 2048], P('dp', 'seq')
- grad_resid: bfloat16 [16, 512, 2048], P('dp', 'seq')
- grad_gate: bfloat16 [24, 2048, 4096], P('seq', None, 'dp')
- grad_up: bfloat16 [24, 2048, 4096], P('seq', None, 'dp')
- grad_down: bfloat16 [24, 4096, 2048], P('seq', 'dp')
The draws below stay inside these ranges and needn't reach their ends.
Inputs may be any that keep to these rules, and one draw needn't show every extreme that they name: `expert_ids`: each token names 2 different experts. Within the tokens of one device (aligned blocks of 64 tokens) no expert is named more than 6 times, a bound that some block reaches. `mem_session`: never falling along the memory rows of one dp index; each of the 4 sessions has 1 to 1024 rows, one exactly 1024. `dec_session`: never falling along the decoder tokens of one dp index; each of the 4 sessions has 1 to 256 tokens, one exactly 256.
All inputs are finite; a program needn't handle non-finite values.
Results may differ from the reference program's by a relative error of at most 0.015.
Values may be sent and summed in bfloat16 or wider, within the bound.
A program may use at most 192 MiB of HBM per device.

```python
import math
import jax
import jax.numpy as jnp
import numpy as np
from jax import lax

D = 2048
FF = 4096
EXPERTS = 24
TOPK = 2
QH = 8
KVH = 2
HD = 128
SESS = 4
DEC_DEV = 64
CAP = 6
MEM_DP = 2048
DEC_DP = 512
MEM_MOST = 1024
DEC_MOST = 256
N_DP = 16
DEVICES = 128


def activation_rows(key, row_count):
    row_shape = (N_DP, row_count, D)
    return jnp.clip(jax.random.normal(key, row_shape, jnp.float32), -6.0, 6.0)


def draw_tokens(key, part):
    key = jax.random.fold_in(key, 21)
    return activation_rows(key, DEC_DP).astype(jnp.bfloat16)


def draw_memory(key, part):
    key = jax.random.fold_in(key, 22)
    return activation_rows(key, MEM_DP).astype(jnp.bfloat16)


def draw_event_bias(key, part):
    key = jax.random.fold_in(key, 11)
    key_base = jax.random.fold_in(key, 0)
    bias_shape = (N_DP, KVH, MEM_DP)
    return jnp.clip(jax.random.normal(key_base, bias_shape, jnp.float32) * 1.5, -6.0, 6.0)


def steps_of(stream_key, shape, shards, smallest, largest):
    level = 1.0
    for dim, blocks in shards:
        draws = jax.random.uniform(jax.random.fold_in(jax.random.fold_in(stream_key, 6), dim), (blocks,), jnp.float32, smallest / len(shards), largest / len(shards))
        level = level * jnp.repeat(jnp.exp(draws), shape[dim] // blocks).reshape((-1,) + (1,) * (len(shape) - 1 - dim))
    return level


def profile(number_of, total, limit, slope):
    loads = [(1 << 20) // math.isqrt(rank ** slope) + 1 for rank in range(2, number_of + 1)]
    surplus, counts = total - limit - (number_of - 1), [1] * (number_of - 1)
    while surplus > 0:
        candidates = [i for i in range(number_of - 1) if counts[i] < limit]
        whole, left = sum([loads[i] for i in candidates]), surplus
        for i in candidates:
            more = min(limit - counts[i], max(1, left * loads[i] // whole), surplus)
            counts[i] = counts[i] + more
            surplus = surplus - more
    return np.array([limit] + counts)


def ragged_sizes(key, number_of, total, most, skew):
    if number_of == 2:
        one = jax.random.randint(key, (), max(1, total - most), min(most, total - 1) + 1)
        return jnp.stack([one, total - one])
    lengths = jnp.asarray(profile(number_of, total, most, skew), jnp.int32)
    pairs = (number_of - 1) // 2
    giver, sink = lengths[1:1 + 2 * pairs:2], lengths[2:2 + 2 * pairs:2]
    room = jnp.minimum(giver - 1, most - sink)
    shifted = jax.random.randint(jax.random.fold_in(key, 1), (pairs,), 0, 1 << 20) % (room + 1)
    lengths = lengths.at[1:1 + 2 * pairs:2].set(giver - shifted).at[2:2 + 2 * pairs:2].set(sink + shifted)
    return lengths[jax.random.permutation(jax.random.fold_in(key, 2), number_of)]


def assign_block(key, own, number, rows, count, top, reach, lean):
    ranking = jax.random.permutation(key, count)
    crowded, usual = shares(count, rows * top, reach, lean, True), shares(count, rows * top, reach, lean, False)
    places = jnp.arange(count)

    def named(tallies, rotation):
        used = int((tallies > 0).sum())
        fixed = max(1, used // 4)
        shifted = fixed + (places - fixed + rotation * (used - fixed)) % max(1, count - fixed)
        return jnp.zeros((count,), jnp.int32).at[ranking[jnp.where(places < fixed, places, shifted)]].set(jnp.asarray(tallies, jnp.int32))

    tallies = jnp.where(number % 4 == 0, named(crowded, number // 4), named(usual, number - number // 4 - 1))
    mixed = jax.random.permutation(jax.random.fold_in(own, 3), count)
    source_of, taker = mixed[0:count // 2 * 2:2], mixed[1:count // 2 * 2:2]
    room = jnp.minimum(tallies[source_of] - 1, reach - tallies[taker]) // 2
    room = jnp.where((source_of == ranking[0]) | (taker == ranking[0]) | (tallies[taker] == 0), 0, jnp.maximum(room, 0))
    shifted = jax.random.randint(jax.random.fold_in(own, 4), (count // 2,), 0, 1 << 20) % (room + 1)
    tallies = tallies.at[source_of].add(-shifted).at[taker].add(shifted)
    items = jnp.searchsorted(jnp.cumsum(tallies), jnp.arange(rows * top), side="right").astype(jnp.int32)
    grid = items.reshape(top, rows).T
    grid = grid[jax.random.permutation(jax.random.fold_in(own, 1), rows)]
    rotation = jax.random.randint(jax.random.fold_in(own, 2), (rows, 1), 0, top)
    return jnp.take_along_axis(grid, (jnp.arange(top)[None, :] + rotation) % top, axis=1)


def shares(amount, total, most, lean, full):
    portions = [(1 << 20) // math.isqrt(standing ** lean) + 1 for standing in range(1, amount + 1)]
    largest = most if full else min(most, max(-(-total // amount), total * portions[0] // sum(portions)))
    least = 1 if total - largest >= amount - 1 else 0
    given, spare = [largest] + [least] * (amount - 1), total - largest - least * (amount - 1)
    while spare > 0:
        movable = [i for i in range(1, amount) if given[i] < largest] or [i for i in range(1, amount) if given[i] < most]
        whole, remaining = sum([portions[i] for i in movable]), spare
        for i in movable:
            addition = min(most - given[i], max(1, remaining * portions[i] // whole), spare)
            given[i] = given[i] + addition
            spare = spare - addition
    return np.array(given)


def normal_values(key, extent, scale, limit, shards=(), kind=jnp.bfloat16):
    loudness = steps_of(key, extent, shards, -0.22, 0.18) if shards else 1.0
    values = jax.random.normal(key, extent, jnp.float32) * scale * loudness
    return jnp.minimum(jnp.maximum(values, -limit), limit).astype(kind)


def setup_inputs(seed: int = 0) -> dict:
    streams_of = jax.random.split(jax.random.key(seed), 16)
    tokens = draw_tokens(jax.random.fold_in(streams_of[15], 71), 0)
    memory = draw_memory(jax.random.fold_in(streams_of[15], 71), 0)
    mem_session = jax.vmap(lambda own: jnp.searchsorted(jnp.cumsum(ragged_sizes(own, SESS, MEM_DP, MEM_MOST, 1)), jnp.arange(MEM_DP), side="right"))(jax.random.split(streams_of[2], N_DP)).reshape((N_DP, MEM_DP)).astype(jnp.int32)
    dec_session = jax.vmap(lambda own: jnp.searchsorted(jnp.cumsum(ragged_sizes(own, SESS, DEC_DP, DEC_MOST, 1)), jnp.arange(DEC_DP), side="right"))(jax.random.split(streams_of[3], N_DP)).reshape((N_DP, DEC_DP)).astype(jnp.int32)
    event_bias = draw_event_bias(jax.random.fold_in(streams_of[15], 71), 0)
    expert_ids_keys = jax.random.split(jax.random.fold_in(streams_of[5], 1), N_DP * DEC_DP // DEC_DEV)
    expert_ids_turns = jax.random.permutation(jax.random.fold_in(streams_of[5], 3), N_DP * DEC_DP // DEC_DEV)
    expert_ids = jax.vmap(lambda own, number: assign_block(jax.random.fold_in(streams_of[5], 2), own, number, DEC_DEV, EXPERTS, TOPK, CAP, 2))(expert_ids_keys, expert_ids_turns).reshape((N_DP, DEC_DP, TOPK))
    route_weights = jnp.clip(0.2 + 0.8 * jax.random.uniform(streams_of[6], (N_DP, DEC_DP, TOPK), jnp.float32) ** steps_of(streams_of[6], (N_DP, DEC_DP, TOPK), ((0, 16), (1, 8)), -0.2, 0.2), 0.2, 1.0)
    norm_gain = jnp.clip(1.0 + 0.15 * jax.random.normal(streams_of[7], (D,), jnp.float32), 0.25, 1.75)
    w_query = normal_values(streams_of[8], (D, QH * HD), D ** -0.5, 0.125, ((0, 8),))
    w_keyval = normal_values(streams_of[9], (D, 2 * KVH * HD), D ** -0.5, 0.125, ((0, 8),))
    w_output = normal_values(streams_of[10], (QH * HD, D), (QH * HD) ** -0.5, 0.1875, ((0, 8),))
    w_gate = normal_values(streams_of[11], (EXPERTS, D, FF), D ** -0.5, 0.125, ((0, 8), (2, 16)))
    w_up = normal_values(streams_of[12], (EXPERTS, D, FF), D ** -0.5, 0.125, ((0, 8), (2, 16)))
    w_down = normal_values(streams_of[13], (EXPERTS, FF, D), FF ** -0.5, 0.09375, ((0, 8), (1, 16)))
    cotangent = normal_values(streams_of[14], (N_DP, DEC_DP, D), 1.0, 6.0, ((0, 16), (1, 8)))
    return dict(tokens=tokens, memory=memory, mem_session=mem_session, dec_session=dec_session, event_bias=event_bias, expert_ids=expert_ids, route_weights=route_weights, norm_gain=norm_gain, w_query=w_query, w_keyval=w_keyval, w_output=w_output, w_gate=w_gate, w_up=w_up, w_down=w_down, cotangent=cotangent)


def rounded(tensor):
    return lax.optimization_barrier(tensor.astype(jnp.bfloat16)).astype(jnp.float32)

def attend(queries, key_rows, value_rows, query_session, memory_session, bias_rows):
    token_count = queries.shape[0]
    query_heads = queries.reshape(token_count, KVH, QH // KVH, HD).astype(jnp.float32)
    key_heads = key_rows.reshape(-1, KVH, HD).astype(jnp.float32)
    value_heads = value_rows.reshape(-1, KVH, HD).astype(jnp.float32)
    scores = jnp.einsum('tkgh,mkh->tkgm', query_heads, key_heads) * HD ** (-0.5)
    scores = scores + bias_rows[None, :, None, :]
    same_session = (query_session[:, None] == memory_session[None, :])[:, None, None, :]
    scores = jnp.where(same_session, scores, -1e+30)
    row_max = lax.optimization_barrier(jnp.max(scores, axis=-1, keepdims=True))
    raised = jnp.exp(scores - row_max)
    probability = (raised / lax.optimization_barrier(jnp.sum(raised, axis=-1, keepdims=True))).astype(jnp.bfloat16)
    attn_mixed = jnp.einsum('tkgm,mkh->tkgh', probability.astype(jnp.float32), value_heads)
    return attn_mixed.astype(jnp.bfloat16).reshape(token_count, QH * HD)

def expert_pass(operands):
    input_rows, grad_rows, gate_weight, up_weight, down_weight = operands
    slice_width = FF // N_DP
    inputs_f = input_rows.astype(jnp.float32)
    grads_f = grad_rows.astype(jnp.float32)
    gate_slices = gate_weight.astype(jnp.float32).reshape(D, N_DP, slice_width)
    up_slices = up_weight.astype(jnp.float32).reshape(D, N_DP, slice_width)
    down_slices = down_weight.astype(jnp.float32).reshape(N_DP, slice_width, D)
    gate_pre = jnp.einsum('rd,dsf->srf', inputs_f, gate_slices)
    up_value = jnp.einsum('rd,dsf->srf', inputs_f, up_slices)
    sigmoid_gate = jax.nn.sigmoid(gate_pre)
    activated = gate_pre * sigmoid_gate
    hidden = rounded(activated * up_value)
    expert_out = lax.optimization_barrier(jnp.sum(rounded(jnp.einsum('srf,sfd->srd', hidden, down_slices)), axis=0)).astype(jnp.bfloat16)
    grad_hidden = jnp.einsum('rd,sfd->srf', grads_f, down_slices)
    grad_gate_pre = rounded(grad_hidden * up_value * sigmoid_gate * (1.0 + gate_pre * (1.0 - sigmoid_gate)))
    grad_up_value = rounded(grad_hidden * activated)
    grad_down = jnp.einsum('srf,rd->sfd', hidden, grads_f).reshape(FF, D).astype(jnp.bfloat16)
    grad_gate = jnp.einsum('rd,srf->dsf', inputs_f, grad_gate_pre).reshape(D, FF).astype(jnp.bfloat16)
    grad_up = jnp.einsum('rd,srf->dsf', inputs_f, grad_up_value).reshape(D, FF).astype(jnp.bfloat16)
    grad_partial = jnp.einsum('srf,dsf->srd', grad_gate_pre, gate_slices) + jnp.einsum('srf,dsf->srd', grad_up_value, up_slices)
    grad_input = lax.optimization_barrier(jnp.sum(rounded(grad_partial), axis=0)).astype(jnp.bfloat16)
    return (expert_out, grad_input, grad_gate, grad_up, grad_down)

def reference(tokens, memory, mem_session, dec_session, event_bias, expert_ids, route_weights, norm_gain, w_query, w_keyval, w_output, w_gate, w_up, w_down, cotangent):
    kv_width = KVH * HD

    def attention_group(operands):
        tokens_group, memory_group, memgroup_session, decgroup_session, bias_group = operands
        queries = jnp.dot(tokens_group, w_query, preferred_element_type=jnp.float32).astype(jnp.bfloat16)
        keyval = jnp.dot(memory_group, w_keyval, preferred_element_type=jnp.float32).astype(jnp.bfloat16)
        attn_mixed = attend(queries, keyval[:, :kv_width], keyval[:, kv_width:], decgroup_session, memgroup_session, bias_group)
        summed = tokens_group.astype(jnp.float32) + jnp.dot(attn_mixed, w_output, preferred_element_type=jnp.float32)
        return summed.astype(jnp.bfloat16)
    residual = lax.map(attention_group, (tokens, memory, mem_session, dec_session, event_bias))
    residual_f = residual.astype(jnp.float32)
    inv_rms = lax.rsqrt(lax.optimization_barrier(jnp.mean(residual_f * residual_f, axis=-1, keepdims=True)) + 1e-05)
    normed = residual_f * inv_rms
    moe_in = (normed * norm_gain).astype(jnp.bfloat16)
    grad_out = (route_weights[..., None] * cotangent.astype(jnp.float32)[..., None, :]).astype(jnp.bfloat16)
    routed = DEC_DEV * TOPK
    flat_experts = expert_ids.reshape(DEVICES, routed).astype(jnp.int32)
    chosen = flat_experts[:, :, None] == jnp.arange(EXPERTS, dtype=jnp.int32)[None, None, :]
    earlier = jnp.cumsum(chosen.astype(jnp.int32), axis=1) - 1
    slot_index = lax.optimization_barrier(jnp.sum(jnp.where(chosen, earlier, 0), axis=2)).astype(jnp.int32)
    column = jnp.arange(DEVICES, dtype=jnp.int32)[:, None] * CAP + slot_index
    input_rows = jnp.repeat(moe_in.reshape(DEVICES, DEC_DEV, D), TOPK, axis=1)
    grad_rows = grad_out.reshape(DEVICES, routed, D)
    input_buffer = jnp.zeros((EXPERTS, DEVICES * CAP, D), jnp.bfloat16).at[flat_experts, column].set(input_rows)
    grad_buffer = jnp.zeros((EXPERTS, DEVICES * CAP, D), jnp.bfloat16).at[flat_experts, column].set(grad_rows)
    expert_results = lax.map(expert_pass, (input_buffer, grad_buffer, w_gate, w_up, w_down))
    out_rows, input_grads, grad_gate, grad_up, grad_down = expert_results
    picked_out = out_rows[flat_experts, column].astype(jnp.float32).reshape(N_DP, DEC_DP, TOPK, D)
    block_out = (residual_f + lax.optimization_barrier(jnp.sum(picked_out * route_weights[..., None], axis=2))).astype(jnp.bfloat16)
    picked_grad = input_grads[flat_experts, column].astype(jnp.float32).reshape(N_DP, DEC_DP, TOPK, D)
    grad_moe = lax.optimization_barrier(jnp.sum(picked_grad, axis=2))
    grad_normed = grad_moe * norm_gain
    correction = normed * lax.optimization_barrier(jnp.mean(grad_normed * normed, axis=-1, keepdims=True))
    grad_resid = (cotangent.astype(jnp.float32) + inv_rms * (grad_normed - correction)).astype(jnp.bfloat16)
    return (block_out, grad_resid, grad_gate, grad_up, grad_down)
```

```python
import functools

import jax
import jax.numpy as jnp
import numpy as np
from jax import lax
from jax.experimental import pallas as pl
from jax.experimental.pallas import tpu as pltpu
from jax.sharding import PartitionSpec as P

D = 2048
EXPERTS = 24
TOPK = 2
QH = 8
KVH = 2
HD = 128
CAP = 6
SIDE = 4
N_DP = 16
N_SEQ = 8
OWN = 3
HID = 256
TOK = 64
SRC = N_SEQ * CAP
BLK = 2 * SRC
PACK = 16
MEM = 256
WIDE = D + 256
KV = 2 * KVH * HD
HALF = D // 2
QUARTER = D // 4
MESH = pl.DeviceIdType.MESH
F32 = jnp.float32
BF16 = jnp.bfloat16
NT = (((1,), (1,)), ((), ()))
TN = (((0,), (0,)), ((), ()))


def return_matrix():
    table = np.zeros((BLK, N_SEQ * PACK), np.float32)
    for kind in range(2):
        for source in range(N_SEQ):
            for slot in range(CAP):
                table[kind * SRC + source * CAP + slot, source * PACK + kind * CAP + slot] = 1.0
    return table


def compact_matrix():
    table = np.zeros((OWN * SRC, OWN * SRC), np.float32)
    for expert in range(OWN):
        for source in range(N_SEQ):
            for slot in range(CAP):
                row = expert * CAP + slot
                column = source * 16 + row if row < 16 else N_SEQ * 16 + source * 2 + row - 16
                table[expert * SRC + source * CAP + slot, column] = 1.0
    return table


def corner_matrix():
    table = np.zeros((N_SEQ * 16, N_SEQ * 16), np.float32)
    for piece in range(8):
        for peer in range(N_SEQ):
            for last in range(2):
                table[peer * 16 + piece * 2 + last, piece * 16 + peer * 2 + last] = 1.0
    return table


def add_rows(out, terms):
    @pl.loop(0, BLK // 16)
    def _(i):
        rows = pl.ds(pl.multiple_of(i * 16, 16), 16)
        total = terms[0][rows, :].astype(F32)
        for term in terms[1:]:
            total = total + term[rows, :].astype(F32)
        out[rows, :] = total.astype(BF16)


def block_kernel(
    tokens_ref,
    meta_ref,
    session_ref,
    cot_ref,
    gain_ref,
    weight_ref,
    place_in_ref,
    place_grad_ref,
    select_ref,
    compact_ref,
    corner_ref,
    corner_back_ref,
    expand_ref,
    memory_hbm,
    query_hbm,
    keyval_hbm,
    output_hbm,
    gate_hbm,
    up_hbm,
    down_hbm,
    block_out_ref,
    grad_resid_ref,
    grad_gate_hbm,
    grad_up_hbm,
    grad_down_hbm,
    rows,
    gate_up,
    down,
    hidden,
    grads,
    stage_gate_up,
    memory,
    meta,
    z_send,
    z_recv,
    back_send,
    back_recv,
    first_far,
    first_near,
    second_far,
    second_near,
    residual_keep,
    own_sem,
    load_sem,
    store_sem,
    m_ssem,
    m_rsem,
    w_ssem,
    w_rsem,
    z_ssem,
    z_rsem,
    b_ssem,
    b_rsem,
    g_ssem,
    g_rsem,
    r_ssem,
    r_rsem,
):
    me = lax.axis_index("dp")
    seq = lax.axis_index("seq")
    mx, my = me // SIDE, me % SIDE
    mz, mc = seq // 2, seq % 2
    stage_down = down.at[OWN]

    def device(half, step1, step2):
        dx, dy = (step1, step2) if half == 0 else (step2, step1)
        return ((mx + dx + SIDE) % SIDE) * SIDE + (my + dy + SIDE) % SIDE

    def columns(half):
        return pl.ds(half * HALF, HALF)

    barrier = pltpu.get_barrier_semaphore()
    for half in range(2):
        for step in (1, -1):
            pl.semaphore_signal(
                barrier, inc=1, device_id=(device(half, step, 0), seq), device_id_type=MESH
            )
    for offset in range(1, N_SEQ):
        pl.semaphore_signal(
            barrier, inc=1, device_id=(me, (seq + offset) % N_SEQ), device_id_type=MESH
        )

    def remote(src, dst, ssem, rsem, target):
        copy = pltpu.make_async_remote_copy(
            src_ref=src,
            dst_ref=dst,
            send_sem=ssem,
            recv_sem=rsem,
            device_id=target,
            device_id_type=MESH,
        )
        copy.start()
        return copy

    own_rows = pl.ds(seq * MEM, MEM)
    own_loads = [
        pltpu.make_async_copy(keyval_hbm, gate_up.at[0, own_rows, :], own_sem.at[0]),
        pltpu.make_async_copy(query_hbm.at[:, pl.ds(0, KV)], gate_up.at[1, own_rows, :], own_sem.at[1]),
        pltpu.make_async_copy(query_hbm.at[:, pl.ds(KV, KV)], gate_up.at[2, own_rows, :], own_sem.at[2]),
        pltpu.make_async_copy(output_hbm, down.at[mz, pl.ds(mc * HD, HD), :], own_sem.at[3]),
        pltpu.make_async_copy(memory_hbm, memory, own_sem.at[4]),
    ]
    for copy in own_loads:
        copy.start()

    z_copies = {}

    def exchange_build(kind, place, sources):
        packed = jnp.dot(place[...], sources, preferred_element_type=F32).astype(BF16)
        z_send[kind, :, :, 0:D] = packed[0 : N_SEQ * 16].reshape(N_SEQ, 16, D)
        last = packed[N_SEQ * 16 :]
        pieces = jnp.concatenate([last[:, i * 256 : (i + 1) * 256] for i in range(8)], axis=0)
        corner = jnp.dot(corner_ref[...], pieces, preferred_element_type=F32).astype(BF16)
        z_send[kind, :, :, D:WIDE] = corner.reshape(N_SEQ, 16, 256)

    def exchange_start(kind):
        for offset in range(1, N_SEQ):
            peer = (seq + offset) % N_SEQ
            z_copies[kind, offset] = remote(
                z_send.at[kind, peer],
                z_recv.at[kind, seq],
                z_ssem.at[kind, offset],
                z_rsem.at[kind, offset],
                (me, peer),
            )
        z_recv[kind, seq] = z_send[kind, seq]

    def exchange_end(kind):
        for offset in range(1, N_SEQ):
            z_copies[kind, offset].wait()
        first = z_recv[kind, :, :, 0:D].reshape(N_SEQ * 16, D)
        corner = z_recv[kind, :, :, D:WIDE].reshape(N_SEQ * 16, 256)
        pieces = jnp.dot(corner_back_ref[...], corner, preferred_element_type=F32).astype(BF16)
        last = jnp.concatenate([pieces[i * 16 : (i + 1) * 16] for i in range(8)], axis=1)
        arrived = jnp.concatenate([first, last], axis=0)
        compact = jnp.dot(compact_ref[...], arrived, preferred_element_type=F32).astype(BF16)
        for e in range(OWN):
            rows[e, me, kind * SRC : (kind + 1) * SRC, :] = compact[e * SRC : (e + 1) * SRC]

    ring = {}

    def keyval_weight_region(zz, cc, start, size):
        return gate_up.at[0, pl.ds((zz * 2 + cc) * MEM + start, size), :]

    def query_weight_region(zz, cc, start, size):
        return gate_up.at[pl.ds(1, 2), pl.ds((zz * 2 + cc) * MEM + start, size), :]

    def output_weight_region(zz, cc, start, size):
        return down.at[zz, pl.ds(cc * HD + start, size), :]

    def keyval_region(zz, cc, start, size):
        return stage_gate_up.at[pl.ds((zz * 2 + cc) * MEM + start, size), :]

    regions = [
        (keyval_weight_region, MEM),
        (query_weight_region, MEM),
        (output_weight_region, HD),
        (keyval_region, MEM),
    ]

    def ring_send(which, index, dz_owner, start, size, step, core):
        ref = regions[which][0]((mz + dz_owner + SIDE) % SIDE, mc, start, size)
        target = (me, ((mz + step + SIDE) % SIDE) * 2 + core)
        ring[which, index] = remote(ref, ref, w_ssem.at[which, index], w_rsem.at[which, index], target)

    def ring_1(which):
        size = regions[which][1]
        ring_send(which, 0, 0, 0, size, 1, mc)
        ring_send(which, 1, 0, 0, size, -1, mc)
        ring_send(which, 4, 0, 0, size, 0, 1 - mc)

    def ring_2(which):
        size = regions[which][1]
        ring[which, 0].wait_recv()
        ring_send(which, 2, -1, 0, size // 2, 1, mc)
        ring_send(which, 5, -1, 0, size, 0, 1 - mc)
        ring[which, 1].wait_recv()
        ring_send(which, 3, 1, size // 2, size // 2, -1, mc)
        ring_send(which, 6, 1, 0, size, 0, 1 - mc)

    def ring_3(which):
        ring[which, 2].wait_recv()
        ring[which, 3].wait_recv()
        ring_send(which, 7, 2, 0, regions[which][1], 0, 1 - mc)

    def ring_4(which):
        for index in range(4, 8):
            ring[which, index].wait_recv()

    def ring_sent(which):
        for index in range(8):
            ring[which, index].wait_send()

    def block(half, r1, r2):
        return device(half, r1, r2)

    gathers = {}

    def gather_send(kind, e, half, index, width, origin, steps):
        target = device(half, *steps)
        part = rows.at[e, origin, pl.ds(kind * SRC, SRC), width]
        copy = remote(part, part, g_ssem.at[kind, e, half, index], g_rsem.at[kind, e, half, index], (target, seq))
        gathers[kind, e, half, index] = copy

    def gather_1(kind, e):
        for half in range(2):
            cols = columns(half)
            gather_send(kind, e, half, 0, cols, me, (1, 0))
            gather_send(kind, e, half, 1, cols, me, (-1, 0))
        for half in range(2):
            cols = columns(half)
            gather_send(kind, e, half, 4, cols, me, (0, 1))
            gather_send(kind, e, half, 8, cols, me, (0, -1))

    def gather_2(kind, e):
        for half in range(2):
            cols = columns(half)
            gathers[kind, e, half, 0].wait_recv()
            gather_send(kind, e, half, 2, pl.ds(half * HALF, QUARTER), block(half, -1, 0), (1, 0))
            gathers[kind, e, half, 1].wait_recv()
            gather_send(kind, e, half, 3, pl.ds(half * HALF + QUARTER, QUARTER), block(half, 1, 0), (-1, 0))
            for r in (1, 3):
                gather_send(kind, e, half, 4 + r, cols, block(half, r, 0), (0, 1))
                gather_send(kind, e, half, 8 + r, cols, block(half, r, 0), (0, -1))

    def gather_3(kind, e):
        for half in range(2):
            cols = columns(half)
            gathers[kind, e, half, 2].wait_recv()
            gathers[kind, e, half, 3].wait_recv()
            gather_send(kind, e, half, 6, cols, block(half, 2, 0), (0, 1))
            gather_send(kind, e, half, 10, cols, block(half, 2, 0), (0, -1))

    def gather_4(kind, e):
        for r in (0, 1, 3, 2):
            for half in range(2):
                cols = columns(half)
                gathers[kind, e, half, 4 + r].wait_recv()
                gathers[kind, e, half, 8 + r].wait_recv()
                if r < 2:
                    gather_send(kind, e, half, 12 + r, cols, block(half, r, -1), (0, 1))
                else:
                    gather_send(kind, e, half, 12 + r, cols, block(half, r, 1), (0, -1))

    def gather_5(kind, e):
        for half in range(2):
            for r in range(4):
                gathers[kind, e, half, 12 + r].wait_recv()
            for index in range(16):
                gathers[kind, e, half, index].wait_send()

    loads = []

    def load_start():
        for e in range(OWN):
            loads.append(
                (
                    pltpu.make_async_copy(gate_hbm.at[e], gate_up.at[e, :, pl.ds(0, HID)], load_sem.at[e, 0]),
                    pltpu.make_async_copy(up_hbm.at[e], gate_up.at[e, :, pl.ds(HID, HID)], load_sem.at[e, 1]),
                    pltpu.make_async_copy(down_hbm.at[e], down.at[e], load_sem.at[e, 2]),
                )
            )
        for group in loads:
            for copy in group:
                copy.start()

    stores = {}

    def compute(e):
        for copy in loads[e]:
            copy.wait()
        if e > 0:
            for copy in stores[e - 1]:
                copy.wait()
        group = 8
        tile = group * SRC

        @pl.loop(0, N_DP // group)
        def _(j):
            blocks = pl.ds(j * group, group)
            out_rows = pl.ds(pl.multiple_of(j * tile, tile), tile)
            inputs = rows[e, blocks, 0:SRC, :].reshape(tile, D)
            both = jnp.dot(inputs, gate_up[e], preferred_element_type=F32)
            outer = rows[e, blocks, SRC:BLK, :].reshape(tile, D)
            grad_hidden = lax.dot_general(outer, down[e], NT, preferred_element_type=F32)
            gate_pre, up_value = both[:, :HID], both[:, HID:]
            sigmoid = jax.nn.sigmoid(gate_pre)
            activated = gate_pre * sigmoid
            hidden[out_rows, :] = (activated * up_value).astype(BF16)
            grads[out_rows, 0:HID] = (
                grad_hidden * up_value * sigmoid * (1.0 + gate_pre * (1.0 - sigmoid))
            ).astype(BF16)
            grads[out_rows, HID : 2 * HID] = (grad_hidden * activated).astype(BF16)

        @pl.loop(0, D // 256)
        def _(j):
            cols = pl.ds(pl.multiple_of(j * 256, 256), 256)
            inputs = rows[e, :, 0:SRC, cols].reshape(N_DP * SRC, 256)
            stage_gate_up[cols, :] = lax.dot_general(
                inputs, grads[...], TN, preferred_element_type=F32
            ).astype(BF16)
            outer = rows[e, :, SRC:BLK, cols].reshape(N_DP * SRC, 256)
            down[OWN, :, cols] = lax.dot_general(
                hidden[...], outer, TN, preferred_element_type=F32
            ).astype(BF16)

        stores[e] = (
            pltpu.make_async_copy(stage_gate_up.at[:, pl.ds(0, HID)], grad_gate_hbm.at[e], store_sem.at[e, 0]),
            pltpu.make_async_copy(stage_gate_up.at[:, pl.ds(HID, HID)], grad_up_hbm.at[e], store_sem.at[e, 1]),
            pltpu.make_async_copy(stage_down, grad_down_hbm.at[e], store_sem.at[e, 2]),
        )
        for copy in stores[e]:
            copy.start()

        @pl.loop(0, D // 256)
        def _(j):
            cols = pl.ds(pl.multiple_of(j * 256, 256), 256)
            out = jnp.dot(hidden[...], down[e, :, cols], preferred_element_type=F32)
            rows[e, :, 0:SRC, cols] = out.astype(BF16).reshape(N_DP, SRC, 256)
            back = lax.dot_general(grads[...], gate_up[e, cols, :], NT, preferred_element_type=F32)
            rows[e, :, SRC:BLK, cols] = back.astype(BF16).reshape(N_DP, SRC, 256)

    reduces = {}

    def reduce_send(e, half, index, src, dst, steps):
        target = device(half, *steps)
        copy = remote(src, dst, r_ssem.at[e, half, index], r_rsem.at[e, half, index], (target, seq))
        reduces[e, half, index] = copy

    def part(e, half, r1, r2):
        return rows.at[e, block(half, r1, r2), :, columns(half)]

    def reduce_1(e):
        for half in range(2):
            for r in range(4):
                step = 1 if r < 2 else -1
                reduce_send(e, half, r, part(e, half, r, 2), first_far.at[e, half, r], (0, step))
        for half in range(2):
            for r in (2, 3):
                reduce_send(e, half, 4 + r, part(e, half, r, 1), first_near.at[e, half, 0, r], (0, 1))
            for r in (0, 1):
                reduce_send(e, half, 8 + r, part(e, half, r, -1), first_near.at[e, half, 1, r], (0, -1))

    def reduce_2(e):
        for r in range(4):
            for half in range(2):
                step = 1 if r < 2 else -1
                reduces[e, half, r].wait_recv()
                mine = part(e, half, r, step)
                add_rows(mine, [mine, first_far.at[e, half, r]])
                way = 0 if r < 2 else 1
                reduce_send(
                    e, half, 4 + 4 * way + r, mine, first_near.at[e, half, way, r], (0, step)
                )

    def reduce_3(e):
        for r in (2, 1, 3, 0):
            for half in range(2):
                reduces[e, half, 4 + r].wait_recv()
                reduces[e, half, 8 + r].wait_recv()
                mine = part(e, half, r, 0)
                add_rows(
                    mine, [mine, first_near.at[e, half, 0, r], first_near.at[e, half, 1, r]]
                )
                if r == 2:
                    for way, step in ((0, 1), (1, -1)):
                        quarter = pl.ds(half * HALF + way * QUARTER, QUARTER)
                        src = rows.at[e, block(half, 2, 0), :, quarter]
                        reduce_send(e, half, 12 + way, src, second_far.at[e, half, way], (step, 0))

    def reduce_4(e):
        for half in range(2):
            for way, step in ((0, 1), (1, -1)):
                reduces[e, half, 12 + way].wait_recv()
                quarter = pl.ds(half * HALF + way * QUARTER, QUARTER)
                mine = rows.at[e, block(half, step, 0), :, quarter]
                add_rows(mine, [mine, second_far.at[e, half, way]])
                reduce_send(
                    e, half, 14 + way, part(e, half, step, 0), second_near.at[e, half, way], (step, 0)
                )

    returned = {}

    def reduce_5(e):
        for half in range(2):
            for way in range(2):
                reduces[e, half, 14 + way].wait_recv()
            mine = part(e, half, 0, 0)
            add_rows(mine, [mine, second_near.at[e, half, 0], second_near.at[e, half, 1]])
        back_send[e] = (
            jnp.dot(expand_ref[...], rows[e, me], preferred_element_type=F32)
            .astype(BF16)
            .reshape(N_SEQ, PACK, D)
        )
        for offset in range(1, N_SEQ):
            peer = (seq + offset) % N_SEQ
            returned[e, offset] = remote(
                back_send.at[e, peer],
                back_recv.at[seq, pl.ds(e * PACK, PACK)],
                b_ssem.at[e, offset],
                b_rsem.at[e, offset],
                (me, peer),
            )
        back_recv[seq, e * PACK : (e + 1) * PACK, :] = back_send[e, seq]

    def attention_part(queries, keys, values, bias, same):
        scores = lax.dot_general(queries, keys, NT, preferred_element_type=F32) * HD ** (-0.5)
        scores = jnp.where(same, scores + bias, -1e30)
        row_max = jnp.max(scores, axis=-1, keepdims=True)
        raised = jnp.exp(scores - row_max)
        probability = (raised / jnp.sum(raised, axis=-1, keepdims=True)).astype(BF16)
        return jnp.dot(probability, values, preferred_element_type=F32).astype(BF16)

    cot = cot_ref[...].astype(F32)
    grad0 = (weight_ref[:, 0:1] * cot).astype(BF16)
    grad1 = (weight_ref[:, 1:2] * cot).astype(BF16)
    exchange_build(1, place_grad_ref, jnp.concatenate([grad0, grad1], axis=0))
    meta[seq] = meta_ref[...]
    own_loads[0].wait()
    pl.semaphore_wait(barrier, 4 + N_SEQ - 1)

    exchange_start(1)
    meta_copies = []
    for offset in range(1, N_SEQ):
        peer = (seq + offset) % N_SEQ
        meta_copies.append(
            remote(meta.at[seq], meta.at[seq], m_ssem.at[offset], m_rsem.at[offset], (me, peer))
        )
    ring_1(0)
    for copy in own_loads[1:]:
        copy.wait()
    ring_2(0)
    ring_1(1)
    exchange_end(1)
    for e in range(OWN):
        gather_1(1, e)
    ring_3(0)
    ring_4(0)
    stage_gate_up[own_rows, :] = jnp.dot(
        memory[...], gate_up[0], preferred_element_type=F32
    ).astype(BF16)
    ring_1(3)
    ring_2(1)
    for e in range(OWN):
        gather_2(1, e)
    ring_2(3)
    ring_1(2)
    ring_3(1)
    for e in range(OWN):
        gather_3(1, e)
    ring_3(3)
    ring_4(1)
    tokens = tokens_ref[...]
    queries = [
        jnp.dot(tokens, gate_up[1 + g], preferred_element_type=F32).astype(BF16) for g in range(KVH)
    ]
    for copy in meta_copies:
        copy.wait()
    ring_4(3)
    session_all = jnp.concatenate([meta[s, 2:3, :] for s in range(N_SEQ)], axis=1)
    same = session_ref[...] == session_all
    mixed = []
    for g in range(KVH):
        keys = stage_gate_up[:, g * HD : (g + 1) * HD]
        values = stage_gate_up[:, (KVH + g) * HD : (KVH + g + 1) * HD]
        bias = jnp.concatenate([meta[s, g : g + 1, :] for s in range(N_SEQ)], axis=1)
        for pair in range(2):
            first = queries[g][:, pair * 2 * HD : (pair * 2 + 1) * HD]
            second = queries[g][:, (pair * 2 + 1) * HD : (pair * 2 + 2) * HD]
            both = attention_part(
                jnp.concatenate([first, second], axis=0), keys, values, bias, same
            )
            mixed.extend([both[0:TOK], both[TOK : 2 * TOK]])
        if g == 0:
            ring_2(2)
    ring_3(2)
    ring_4(2)
    mixed = jnp.concatenate(mixed, axis=1)
    projected = jnp.dot(
        mixed, down[...].reshape((OWN + 1) * HID, D), preferred_element_type=F32
    )
    residual_keep[...] = (tokens.astype(F32) + projected).astype(BF16)
    residual = residual_keep[...].astype(F32)
    inv_rms = lax.rsqrt(jnp.mean(residual * residual, axis=-1, keepdims=True) + 1e-05)
    moe_in = (residual * inv_rms * gain_ref[...]).astype(BF16)
    exchange_build(0, place_in_ref, moe_in)
    exchange_start(0)
    for which in range(4):
        ring_sent(which)
    load_start()
    for e in range(OWN):
        gather_4(1, e)
    exchange_end(0)
    for e in range(OWN):
        gather_1(0, e)
    for e in range(OWN):
        gather_2(0, e)
    for e in range(OWN):
        gather_3(0, e)
    for e in range(OWN):
        gather_5(1, e)
    gather_4(0, 0)
    gather_5(0, 0)
    compute(0)
    gather_4(0, 1)
    reduce_1(0)
    gather_5(0, 1)
    compute(1)
    gather_4(0, 2)
    reduce_2(0)
    reduce_1(1)
    gather_5(0, 2)
    compute(2)
    reduce_1(2)
    reduce_2(1)
    reduce_3(0)
    reduce_2(2)
    reduce_4(0)
    reduce_3(1)
    reduce_5(0)
    reduce_4(1)
    reduce_3(2)
    reduce_4(2)
    reduce_5(1)
    reduce_5(2)
    for copy in returned.values():
        copy.wait()
    for copy in reduces.values():
        copy.wait_send()
    for copy in stores[OWN - 1]:
        copy.wait()

    back = back_recv[...].reshape(N_SEQ * OWN * PACK, D)
    picked = jnp.dot(select_ref[...], back, preferred_element_type=F32)
    residual = residual_keep[...].astype(F32)
    block_out_ref[...] = (
        residual
        + (picked[0:TOK] * weight_ref[:, 0:1] + picked[TOK : 2 * TOK] * weight_ref[:, 1:2])
    ).astype(BF16)
    inv_rms = lax.rsqrt(jnp.mean(residual * residual, axis=-1, keepdims=True) + 1e-05)
    normed = residual * inv_rms
    grad_normed = picked[2 * TOK :] * gain_ref[...]
    correction = normed * jnp.mean(grad_normed * normed, axis=-1, keepdims=True)
    grad_resid_ref[...] = (
        cot_ref[...].astype(F32) + inv_rms * (grad_normed - correction)
    ).astype(BF16)


def decoder_block(tokens, memory, meta, session, cot, gain, weights, places, projections, experts):
    vmem = pl.BlockSpec(memory_space=pltpu.VMEM)
    hbm = pl.BlockSpec(memory_space=pl.ANY)
    corner = corner_matrix()
    dma = pltpu.SemaphoreType.DMA
    return pl.pallas_call(
        block_kernel,
        out_shape=(
            jax.ShapeDtypeStruct((TOK, D), BF16),
            jax.ShapeDtypeStruct((TOK, D), BF16),
        )
        + tuple(jax.ShapeDtypeStruct(w.shape, BF16) for w in experts),
        in_specs=[vmem] * 13 + [hbm] * 7,
        out_specs=(vmem, vmem, hbm, hbm, hbm),
        scratch_shapes=[
            pltpu.VMEM((OWN, N_DP, BLK, D), BF16),
            pltpu.VMEM((OWN, D, 2 * HID), BF16),
            pltpu.VMEM((OWN + 1, HID, D), BF16),
            pltpu.VMEM((N_DP * SRC, HID), BF16),
            pltpu.VMEM((N_DP * SRC, 2 * HID), BF16),
            pltpu.VMEM((D, 2 * HID), BF16),
            pltpu.VMEM((MEM, D), BF16),
            pltpu.VMEM((N_SEQ, 8, MEM), F32),
            pltpu.VMEM((2, N_SEQ, 16, WIDE), BF16),
            pltpu.VMEM((2, N_SEQ, 16, WIDE), BF16),
            pltpu.VMEM((OWN, N_SEQ, PACK, D), BF16),
            pltpu.VMEM((N_SEQ, OWN * PACK, D), BF16),
            pltpu.VMEM((OWN, 2, 4, BLK, HALF), BF16),
            pltpu.VMEM((OWN, 2, 2, 4, BLK, HALF), BF16),
            pltpu.VMEM((OWN, 2, 2, BLK, QUARTER), BF16),
            pltpu.VMEM((OWN, 2, 2, BLK, HALF), BF16),
            pltpu.VMEM((TOK, D), BF16),
            dma((5,)),
            dma((OWN, 3)),
            dma((OWN, 3)),
            dma((N_SEQ,)),
            dma((N_SEQ,)),
            dma((4, 8)),
            dma((4, 8)),
            dma((2, N_SEQ)),
            dma((2, N_SEQ)),
            dma((OWN, N_SEQ)),
            dma((OWN, N_SEQ)),
            dma((2, OWN, 2, 16)),
            dma((2, OWN, 2, 16)),
            dma((OWN, 2, 16)),
            dma((OWN, 2, 16)),
        ],
        compiler_params=pltpu.CompilerParams(
            collective_id=1, has_side_effects=True, vmem_limit_bytes=63 * 2**20
        ),
        name="decoder_block",
    )(
        tokens,
        meta,
        session,
        cot,
        gain.reshape(1, D),
        weights,
        *places,
        jnp.asarray(compact_matrix(), BF16),
        jnp.asarray(corner, BF16),
        jnp.asarray(corner.T, BF16),
        jnp.asarray(return_matrix().T, BF16),
        memory,
        *projections,
        *experts,
    )


def routing(expert_ids):
    flat = expert_ids.reshape(-1)
    chosen = flat[:, None] == jnp.arange(EXPERTS, dtype=jnp.int32)[None, :]
    earlier = jnp.cumsum(chosen.astype(jnp.int32), axis=0) - 1
    slot = jnp.sum(jnp.where(chosen, earlier, 0), axis=1)
    owner, place = flat // OWN, (flat % OWN) * CAP + slot
    row = jnp.where(place < 16, owner * 16 + place, N_SEQ * 16 + owner * 2 + place - 16)
    row = row.reshape(-1, TOPK)
    every = jnp.arange(N_SEQ * 18, dtype=jnp.int32)
    sent = [every[:, None] == row[None, :, k] for k in range(TOPK)]
    place_in = (sent[0] | sent[1]).astype(BF16)
    place_grad = jnp.concatenate(sent, axis=1).astype(BF16)
    back = (flat * PACK + slot).reshape(-1, TOPK)
    every = jnp.arange(EXPERTS * PACK, dtype=jnp.int32)
    hit = [every[None, :] == back[:, k : k + 1] for k in range(TOPK)]
    hit_grad = [every[None, :] == back[:, k : k + 1] + CAP for k in range(TOPK)]
    select = jnp.concatenate([hit[0], hit[1], hit_grad[0] | hit_grad[1]], axis=0).astype(BF16)
    return place_in, place_grad, select


def per_device(
    tokens,
    memory,
    mem_session,
    dec_session,
    event_bias,
    expert_ids,
    route_weights,
    norm_gain,
    w_query,
    w_keyval,
    w_output,
    w_gate,
    w_up,
    w_down,
    cotangent,
):
    meta = jnp.concatenate(
        [event_bias[0], mem_session.astype(F32), jnp.zeros((8 - KVH - 1, MEM), F32)], axis=0
    )
    session = jnp.tile(dec_session[0].astype(F32), 2).reshape(2 * TOK, 1)
    block_out, grad_resid, grad_gate, grad_up, grad_down = decoder_block(
        tokens[0],
        memory[0],
        meta,
        session,
        cotangent[0],
        norm_gain,
        route_weights[0],
        routing(expert_ids[0]),
        (w_query, w_keyval, w_output),
        (w_gate, w_up, w_down),
    )
    return (block_out[None], grad_resid[None], grad_gate, grad_up, grad_down)


def solution(mesh):
    return jax.shard_map(
        per_device,
        mesh=mesh,
        in_specs=(
            P("dp", "seq", None),
            P("dp", "seq", None),
            P("dp", "seq"),
            P("dp", "seq"),
            P("dp", None, "seq"),
            P("dp", "seq", None),
            P("dp", "seq", None),
            P(),
            P("seq", None),
            P("seq", None),
            P("seq", None),
            P("seq", None, "dp"),
            P("seq", None, "dp"),
            P("seq", "dp", None),
            P("dp", "seq", None),
        ),
        out_specs=(
            P("dp", "seq", None),
            P("dp", "seq", None),
            P("seq", None, "dp"),
            P("seq", None, "dp"),
            P("seq", "dp", None),
        ),
        check_vma=False,
    )
```

```python
import functools

import jax
import jax.numpy as jnp
import numpy as np
from jax import lax
from jax.experimental import pallas as pl
from jax.experimental.pallas import tpu as pltpu
from jax.sharding import PartitionSpec as P

D = 2048
EXPERTS = 24
TOPK = 2
QH = 8
KVH = 2
HD = 128
CAP = 6
SIDE = 4
N_DP = 16
N_SEQ = 8
OWN = 3
HID = 256
TOK = 64
SRC = N_SEQ * CAP
BLK = 2 * SRC
PACK = 16
MEM = 256
WIDE = D + 256
KV = 2 * KVH * HD
HALF = D // 2
QUARTER = D // 4
MESH = pl.DeviceIdType.MESH
F32 = jnp.float32
BF16 = jnp.bfloat16
NT = (((1,), (1,)), ((), ()))
TN = (((0,), (0,)), ((), ()))


def return_matrix():
    table = np.zeros((BLK, N_SEQ * PACK), np.float32)
    for kind in range(2):
        for source in range(N_SEQ):
            for slot in range(CAP):
                table[kind * SRC + source * CAP + slot, source * PACK + kind * CAP + slot] = 1.0
    return table


def compact_matrix():
    table = np.zeros((OWN * SRC, OWN * SRC), np.float32)
    for expert in range(OWN):
        for source in range(N_SEQ):
            for slot in range(CAP):
                row = expert * CAP + slot
                column = source * 16 + row if row < 16 else N_SEQ * 16 + source * 2 + row - 16
                table[expert * SRC + source * CAP + slot, column] = 1.0
    return table


def corner_matrix():
    table = np.zeros((N_SEQ * 16, N_SEQ * 16), np.float32)
    for piece in range(8):
        for peer in range(N_SEQ):
            for last in range(2):
                table[peer * 16 + piece * 2 + last, piece * 16 + peer * 2 + last] = 1.0
    return table


def squares():
    down = lax.broadcasted_iota(jnp.int32, (TOK, TOK), 0)
    across = lax.broadcasted_iota(jnp.int32, (TOK, TOK), 1)
    return down, across


def as_column(row):
    down, across = squares()
    return jnp.sum(jnp.where(down == across, row, 0.0), axis=1, keepdims=True)


def one_hot(mask):
    return jnp.where(mask, 1.0, 0.0).astype(BF16)


def routed(ids_ref):
    down, across = squares()
    row = [ids_ref[k : k + 1, :].astype(F32) for k in range(TOPK)]
    column = [as_column(r) for r in row]

    def earlier(own, others, before, axis):
        named = sum(jnp.where(own == other, 1.0, 0.0) for other in others)
        return jnp.sum(jnp.where(before, named, 0.0), axis=axis, keepdims=True)

    row_slot = [earlier(row[k], column, down < across, 0) for k in range(TOPK)]
    column_slot = [earlier(column[k], row, across < down, 1) for k in range(TOPK)]
    return row, row_slot, column, column_slot


def send_places(ids_ref):
    row, row_slot, _, _ = routed(ids_ref)
    every = lax.broadcasted_iota(jnp.int32, (N_SEQ * 18, TOK), 0).astype(F32)
    places = []
    for k in range(TOPK):
        owner = jnp.floor((row[k] + 0.5) * (1.0 / OWN))
        place = (row[k] - OWN * owner) * CAP + row_slot[k]
        target = jnp.where(
            place < 16, owner * 16 + place, N_SEQ * 16 + owner * 2 + place - 16
        )
        places.append(jnp.where(every == target, 1.0, 0.0))
    return places


def add_rows(out, terms):
    @pl.loop(0, BLK // 16)
    def _(i):
        rows = pl.ds(pl.multiple_of(i * 16, 16), 16)
        total = terms[0][rows, :].astype(F32)
        for term in terms[1:]:
            total = total + term[rows, :].astype(F32)
        out[rows, :] = total.astype(BF16)


def finish_kernel(
    ids_ref,
    weight_ref,
    back_ref,
    residual_ref,
    cot_ref,
    gain_ref,
    gate_in,
    up_in,
    down_in,
    block_out_ref,
    grad_resid_ref,
    gate_out,
    up_out,
    down_out,
    sem,
):
    copies = []
    for e in range(OWN):
        for i, (src, dst) in enumerate(((gate_in, gate_out), (up_in, up_out), (down_in, down_out))):
            copies.append(pltpu.make_async_copy(src.at[e], dst.at[e], sem.at[e, i]))
    for copy in copies:
        copy.start()
    _, _, column, column_slot = routed(ids_ref)
    every = lax.broadcasted_iota(jnp.int32, (TOK, EXPERTS * PACK), 1).astype(F32)
    back = back_ref[...].reshape(EXPERTS * PACK, D)
    answers = [column[k] * PACK + column_slot[k] for k in range(TOPK)]
    residual = residual_ref[...].astype(F32)
    combined = None
    for k in range(TOPK):
        picked = jnp.dot(one_hot(every == answers[k]), back, preferred_element_type=F32)
        term = picked * as_column(weight_ref[k : k + 1, :])
        combined = term if combined is None else combined + term
    block_out_ref[...] = (residual + combined).astype(BF16)
    both = (every == answers[0] + CAP) | (every == answers[1] + CAP)
    grad_moe = jnp.dot(one_hot(both), back, preferred_element_type=F32)
    inv_rms = lax.rsqrt(jnp.mean(residual * residual, axis=-1, keepdims=True) + 1e-05)
    normed = residual * inv_rms
    grad_normed = grad_moe * gain_ref[...]
    correction = normed * jnp.mean(grad_normed * normed, axis=-1, keepdims=True)
    grad_resid_ref[...] = (
        cot_ref[...].astype(F32) + inv_rms * (grad_normed - correction)
    ).astype(BF16)
    for copy in copies:
        copy.wait()


def block_kernel(
    tokens_ref,
    bias_ref,
    mem_session_ref,
    session_ref,
    cot_ref,
    gain_ref,
    ids_ref,
    weight_ref,
    compact_ref,
    corner_ref,
    corner_back_ref,
    expand_ref,
    memory_hbm,
    query_hbm,
    keyval_hbm,
    output_hbm,
    gate_hbm,
    up_hbm,
    down_hbm,
    back_recv,
    residual_keep,
    grad_gate_hbm,
    grad_up_hbm,
    grad_down_hbm,
    rows,
    gate_up,
    down,
    hidden,
    grads,
    stage_gate_up,
    memory,
    meta,
    z_send,
    z_recv,
    back_send,
    first_far,
    first_near,
    second_far,
    second_near,
    own_sem,
    load_sem,
    store_sem,
    m_ssem,
    m_rsem,
    w_ssem,
    w_rsem,
    z_ssem,
    z_rsem,
    b_ssem,
    b_rsem,
    g_ssem,
    g_rsem,
    r_ssem,
    r_rsem,
):
    me = lax.axis_index("dp")
    seq = lax.axis_index("seq")
    mx, my = me // SIDE, me % SIDE
    mz, mc = seq // 2, seq % 2
    stage_down = down.at[OWN]

    def device(half, step1, step2):
        dx, dy = (step1, step2) if half == 0 else (step2, step1)
        return ((mx + dx + SIDE) % SIDE) * SIDE + (my + dy + SIDE) % SIDE

    def columns(half):
        return pl.ds(half * HALF, HALF)

    barrier = pltpu.get_barrier_semaphore()
    for half in range(2):
        for step in (1, -1):
            pl.semaphore_signal(
                barrier, inc=1, device_id=(device(half, step, 0), seq), device_id_type=MESH
            )
    for offset in range(1, N_SEQ):
        pl.semaphore_signal(
            barrier, inc=1, device_id=(me, (seq + offset) % N_SEQ), device_id_type=MESH
        )

    def remote(src, dst, ssem, rsem, target):
        copy = pltpu.make_async_remote_copy(
            src_ref=src,
            dst_ref=dst,
            send_sem=ssem,
            recv_sem=rsem,
            device_id=target,
            device_id_type=MESH,
        )
        copy.start()
        return copy

    own_rows = pl.ds(seq * MEM, MEM)
    own_loads = [
        pltpu.make_async_copy(keyval_hbm, gate_up.at[0, own_rows, :], own_sem.at[0]),
        pltpu.make_async_copy(query_hbm.at[:, pl.ds(0, KV)], gate_up.at[1, own_rows, :], own_sem.at[1]),
        pltpu.make_async_copy(query_hbm.at[:, pl.ds(KV, KV)], gate_up.at[2, own_rows, :], own_sem.at[2]),
        pltpu.make_async_copy(output_hbm, down.at[mz, pl.ds(mc * HD, HD), :], own_sem.at[3]),
        pltpu.make_async_copy(memory_hbm, memory, own_sem.at[4]),
    ]
    for copy in own_loads:
        copy.start()

    z_copies = {}

    def exchange_build(kind, packed):
        z_send[kind, :, :, 0:D] = packed[0 : N_SEQ * 16].reshape(N_SEQ, 16, D)
        last = packed[N_SEQ * 16 :]
        pieces = jnp.concatenate([last[:, i * 256 : (i + 1) * 256] for i in range(8)], axis=0)
        corner = jnp.dot(corner_ref[...], pieces, preferred_element_type=F32).astype(BF16)
        z_send[kind, :, :, D:WIDE] = corner.reshape(N_SEQ, 16, 256)

    def exchange_start(kind):
        for offset in range(1, N_SEQ):
            peer = (seq + offset) % N_SEQ
            z_copies[kind, offset] = remote(
                z_send.at[kind, peer],
                z_recv.at[kind, seq],
                z_ssem.at[kind, offset],
                z_rsem.at[kind, offset],
                (me, peer),
            )
        z_recv[kind, seq] = z_send[kind, seq]

    def exchange_end(kind):
        for offset in range(1, N_SEQ):
            z_copies[kind, offset].wait()
        first = z_recv[kind, :, :, 0:D].reshape(N_SEQ * 16, D)
        corner = z_recv[kind, :, :, D:WIDE].reshape(N_SEQ * 16, 256)
        pieces = jnp.dot(corner_back_ref[...], corner, preferred_element_type=F32).astype(BF16)
        last = jnp.concatenate([pieces[i * 16 : (i + 1) * 16] for i in range(8)], axis=1)
        arrived = jnp.concatenate([first, last], axis=0)
        compact = jnp.dot(compact_ref[...], arrived, preferred_element_type=F32).astype(BF16)
        for e in range(OWN):
            rows[e, me, kind * SRC : (kind + 1) * SRC, :] = compact[e * SRC : (e + 1) * SRC]

    ring = {}

    def keyval_weight_region(zz, cc, start, size):
        return gate_up.at[0, pl.ds((zz * 2 + cc) * MEM + start, size), :]

    def query_weight_region(zz, cc, start, size):
        return gate_up.at[pl.ds(1, 2), pl.ds((zz * 2 + cc) * MEM + start, size), :]

    def output_weight_region(zz, cc, start, size):
        return down.at[zz, pl.ds(cc * HD + start, size), :]

    def keyval_region(zz, cc, start, size):
        return stage_gate_up.at[pl.ds((zz * 2 + cc) * MEM + start, size), :]

    regions = [
        (keyval_weight_region, MEM),
        (query_weight_region, MEM),
        (output_weight_region, HD),
        (keyval_region, MEM),
    ]

    def ring_send(which, index, dz_owner, start, size, step, core):
        ref = regions[which][0]((mz + dz_owner + SIDE) % SIDE, mc, start, size)
        target = (me, ((mz + step + SIDE) % SIDE) * 2 + core)
        ring[which, index] = remote(ref, ref, w_ssem.at[which, index], w_rsem.at[which, index], target)

    def ring_1(which):
        size = regions[which][1]
        ring_send(which, 0, 0, 0, size, 1, mc)
        ring_send(which, 1, 0, 0, size, -1, mc)
        ring_send(which, 4, 0, 0, size, 0, 1 - mc)

    def ring_2(which):
        size = regions[which][1]
        ring[which, 0].wait_recv()
        ring_send(which, 2, -1, 0, size // 2, 1, mc)
        ring_send(which, 5, -1, 0, size, 0, 1 - mc)
        ring[which, 1].wait_recv()
        ring_send(which, 3, 1, size // 2, size // 2, -1, mc)
        ring_send(which, 6, 1, 0, size, 0, 1 - mc)

    def ring_3(which):
        ring[which, 2].wait_recv()
        ring[which, 3].wait_recv()
        ring_send(which, 7, 2, 0, regions[which][1], 0, 1 - mc)

    def ring_4(which):
        for index in range(4, 8):
            ring[which, index].wait_recv()

    def ring_sent(which):
        for index in range(8):
            ring[which, index].wait_send()

    def block(half, r1, r2):
        return device(half, r1, r2)

    gathers = {}

    def gather_send(kind, e, half, index, width, origin, steps):
        target = device(half, *steps)
        part = rows.at[e, origin, pl.ds(kind * SRC, SRC), width]
        copy = remote(part, part, g_ssem.at[kind, e, half, index], g_rsem.at[kind, e, half, index], (target, seq))
        gathers[kind, e, half, index] = copy

    def gather_1(kind, e):
        for half in range(2):
            cols = columns(half)
            gather_send(kind, e, half, 0, cols, me, (1, 0))
            gather_send(kind, e, half, 1, cols, me, (-1, 0))
        for half in range(2):
            cols = columns(half)
            gather_send(kind, e, half, 4, cols, me, (0, 1))
            gather_send(kind, e, half, 8, cols, me, (0, -1))

    def gather_2(kind, e):
        for half in range(2):
            cols = columns(half)
            gathers[kind, e, half, 0].wait_recv()
            gather_send(kind, e, half, 2, pl.ds(half * HALF, QUARTER), block(half, -1, 0), (1, 0))
            gathers[kind, e, half, 1].wait_recv()
            gather_send(kind, e, half, 3, pl.ds(half * HALF + QUARTER, QUARTER), block(half, 1, 0), (-1, 0))
            for r in (1, 3):
                gather_send(kind, e, half, 4 + r, cols, block(half, r, 0), (0, 1))
                gather_send(kind, e, half, 8 + r, cols, block(half, r, 0), (0, -1))

    def gather_3(kind, e):
        for half in range(2):
            cols = columns(half)
            gathers[kind, e, half, 2].wait_recv()
            gathers[kind, e, half, 3].wait_recv()
            gather_send(kind, e, half, 6, cols, block(half, 2, 0), (0, 1))
            gather_send(kind, e, half, 10, cols, block(half, 2, 0), (0, -1))

    def gather_4(kind, e):
        for r in (0, 1, 3, 2):
            for half in range(2):
                cols = columns(half)
                gathers[kind, e, half, 4 + r].wait_recv()
                gathers[kind, e, half, 8 + r].wait_recv()
                if r < 2:
                    gather_send(kind, e, half, 12 + r, cols, block(half, r, -1), (0, 1))
                else:
                    gather_send(kind, e, half, 12 + r, cols, block(half, r, 1), (0, -1))

    def gather_5(kind, e):
        for half in range(2):
            for r in range(4):
                gathers[kind, e, half, 12 + r].wait_recv()
            for index in range(16):
                gathers[kind, e, half, index].wait_send()

    loads = []

    def load_start():
        for e in range(OWN):
            loads.append(
                (
                    pltpu.make_async_copy(gate_hbm.at[e], gate_up.at[e, :, pl.ds(0, HID)], load_sem.at[e, 0]),
                    pltpu.make_async_copy(up_hbm.at[e], gate_up.at[e, :, pl.ds(HID, HID)], load_sem.at[e, 1]),
                    pltpu.make_async_copy(down_hbm.at[e], down.at[e], load_sem.at[e, 2]),
                )
            )
        for group in loads:
            for copy in group:
                copy.start()

    stores = {}

    def compute(e):
        for copy in loads[e]:
            copy.wait()
        if e > 0:
            for copy in stores[e - 1]:
                copy.wait()
        group = 8
        tile = group * SRC

        @pl.loop(0, N_DP // group)
        def _(j):
            blocks = pl.ds(j * group, group)
            out_rows = pl.ds(pl.multiple_of(j * tile, tile), tile)
            inputs = rows[e, blocks, 0:SRC, :].reshape(tile, D)
            both = jnp.dot(inputs, gate_up[e], preferred_element_type=F32)
            outer = rows[e, blocks, SRC:BLK, :].reshape(tile, D)
            grad_hidden = lax.dot_general(outer, down[e], NT, preferred_element_type=F32)
            gate_pre, up_value = both[:, :HID], both[:, HID:]
            sigmoid = jax.nn.sigmoid(gate_pre)
            activated = gate_pre * sigmoid
            hidden[out_rows, :] = (activated * up_value).astype(BF16)
            grads[out_rows, 0:HID] = (
                grad_hidden * up_value * sigmoid * (1.0 + gate_pre * (1.0 - sigmoid))
            ).astype(BF16)
            grads[out_rows, HID : 2 * HID] = (grad_hidden * activated).astype(BF16)

        @pl.loop(0, D // 256)
        def _(j):
            cols = pl.ds(pl.multiple_of(j * 256, 256), 256)
            inputs = rows[e, :, 0:SRC, cols].reshape(N_DP * SRC, 256)
            stage_gate_up[cols, :] = lax.dot_general(
                inputs, grads[...], TN, preferred_element_type=F32
            ).astype(BF16)
            outer = rows[e, :, SRC:BLK, cols].reshape(N_DP * SRC, 256)
            down[OWN, :, cols] = lax.dot_general(
                hidden[...], outer, TN, preferred_element_type=F32
            ).astype(BF16)

        stores[e] = (
            pltpu.make_async_copy(stage_gate_up.at[:, pl.ds(0, HID)], grad_gate_hbm.at[e], store_sem.at[e, 0]),
            pltpu.make_async_copy(stage_gate_up.at[:, pl.ds(HID, HID)], grad_up_hbm.at[e], store_sem.at[e, 1]),
            pltpu.make_async_copy(stage_down, grad_down_hbm.at[e], store_sem.at[e, 2]),
        )
        for copy in stores[e]:
            copy.start()

        @pl.loop(0, D // 256)
        def _(j):
            cols = pl.ds(pl.multiple_of(j * 256, 256), 256)
            out = jnp.dot(hidden[...], down[e, :, cols], preferred_element_type=F32)
            rows[e, :, 0:SRC, cols] = out.astype(BF16).reshape(N_DP, SRC, 256)
            back = lax.dot_general(grads[...], gate_up[e, cols, :], NT, preferred_element_type=F32)
            rows[e, :, SRC:BLK, cols] = back.astype(BF16).reshape(N_DP, SRC, 256)

    reduces = {}

    def reduce_send(e, half, index, src, dst, steps):
        target = device(half, *steps)
        copy = remote(src, dst, r_ssem.at[e, half, index], r_rsem.at[e, half, index], (target, seq))
        reduces[e, half, index] = copy

    def part(e, half, r1, r2):
        return rows.at[e, block(half, r1, r2), :, columns(half)]

    def reduce_1(e):
        for half in range(2):
            for r in range(4):
                step = 1 if r < 2 else -1
                reduce_send(e, half, r, part(e, half, r, 2), first_far.at[e, half, r], (0, step))
        for half in range(2):
            for r in (2, 3):
                reduce_send(e, half, 4 + r, part(e, half, r, 1), first_near.at[e, half, 0, r], (0, 1))
            for r in (0, 1):
                reduce_send(e, half, 8 + r, part(e, half, r, -1), first_near.at[e, half, 1, r], (0, -1))

    def reduce_2(e):
        for r in range(4):
            for half in range(2):
                step = 1 if r < 2 else -1
                reduces[e, half, r].wait_recv()
                mine = part(e, half, r, step)
                add_rows(mine, [mine, first_far.at[e, half, r]])
                way = 0 if r < 2 else 1
                reduce_send(
                    e, half, 4 + 4 * way + r, mine, first_near.at[e, half, way, r], (0, step)
                )

    def reduce_3(e):
        for r in (2, 1, 3, 0):
            for half in range(2):
                reduces[e, half, 4 + r].wait_recv()
                reduces[e, half, 8 + r].wait_recv()
                mine = part(e, half, r, 0)
                add_rows(
                    mine, [mine, first_near.at[e, half, 0, r], first_near.at[e, half, 1, r]]
                )
                if r == 2:
                    for way, step in ((0, 1), (1, -1)):
                        quarter = pl.ds(half * HALF + way * QUARTER, QUARTER)
                        src = rows.at[e, block(half, 2, 0), :, quarter]
                        reduce_send(e, half, 12 + way, src, second_far.at[e, half, way], (step, 0))

    def reduce_4(e):
        for half in range(2):
            for way, step in ((0, 1), (1, -1)):
                reduces[e, half, 12 + way].wait_recv()
                quarter = pl.ds(half * HALF + way * QUARTER, QUARTER)
                mine = rows.at[e, block(half, step, 0), :, quarter]
                add_rows(mine, [mine, second_far.at[e, half, way]])
                reduce_send(
                    e, half, 14 + way, part(e, half, step, 0), second_near.at[e, half, way], (step, 0)
                )

    returned = {}

    def reduce_5(e):
        for half in range(2):
            for way in range(2):
                reduces[e, half, 14 + way].wait_recv()
            mine = part(e, half, 0, 0)
            add_rows(mine, [mine, second_near.at[e, half, 0], second_near.at[e, half, 1]])
        back_send[e] = (
            jnp.dot(expand_ref[...], rows[e, me], preferred_element_type=F32)
            .astype(BF16)
            .reshape(N_SEQ, PACK, D)
        )
        for offset in range(1, N_SEQ):
            peer = (seq + offset) % N_SEQ
            returned[e, offset] = remote(
                back_send.at[e, peer],
                back_recv.at[seq, pl.ds(e * PACK, PACK)],
                b_ssem.at[e, offset],
                b_rsem.at[e, offset],
                (me, peer),
            )
        back_recv[seq, e * PACK : (e + 1) * PACK, :] = back_send[e, seq]

    def attention_part(queries, keys, values, bias, same):
        scores = lax.dot_general(queries, keys, NT, preferred_element_type=F32) * HD ** (-0.5)
        scores = jnp.where(same, scores + bias, -1e30)
        row_max = jnp.max(scores, axis=-1, keepdims=True)
        raised = jnp.exp(scores - row_max)
        probability = (raised / jnp.sum(raised, axis=-1, keepdims=True)).astype(BF16)
        return jnp.dot(probability, values, preferred_element_type=F32).astype(BF16)

    places = send_places(ids_ref)
    cot = cot_ref[...].astype(F32)
    packed = None
    for k in range(TOPK):
        grad_out = (as_column(weight_ref[k : k + 1, :]) * cot).astype(BF16)
        term = jnp.dot(places[k].astype(BF16), grad_out, preferred_element_type=F32)
        packed = term if packed is None else packed + term
    exchange_build(1, packed.astype(BF16))
    meta[seq] = jnp.concatenate(
        [bias_ref[...], mem_session_ref[...].astype(F32), jnp.zeros((8 - KVH - 1, MEM), F32)],
        axis=0,
    )
    own_loads[0].wait()
    pl.semaphore_wait(barrier, 4 + N_SEQ - 1)

    exchange_start(1)
    meta_copies = []
    for offset in range(1, N_SEQ):
        peer = (seq + offset) % N_SEQ
        meta_copies.append(
            remote(meta.at[seq], meta.at[seq], m_ssem.at[offset], m_rsem.at[offset], (me, peer))
        )
    ring_1(0)
    for copy in own_loads[1:]:
        copy.wait()
    ring_2(0)
    ring_1(1)
    exchange_end(1)
    for e in range(OWN):
        gather_1(1, e)
    ring_3(0)
    ring_4(0)
    stage_gate_up[own_rows, :] = jnp.dot(
        memory[...], gate_up[0], preferred_element_type=F32
    ).astype(BF16)
    ring_1(3)
    ring_2(1)
    for e in range(OWN):
        gather_2(1, e)
    ring_2(3)
    ring_1(2)
    ring_3(1)
    for e in range(OWN):
        gather_3(1, e)
    ring_3(3)
    ring_4(1)
    tokens = tokens_ref[...]
    queries = [
        jnp.dot(tokens, gate_up[1 + g], preferred_element_type=F32).astype(BF16) for g in range(KVH)
    ]
    for copy in meta_copies:
        copy.wait()
    ring_4(3)
    session_all = jnp.concatenate([meta[s, 2:3, :] for s in range(N_SEQ)], axis=1)
    own_session = as_column(session_ref[...].astype(F32))
    same = jnp.concatenate([own_session, own_session], axis=0) == session_all
    mixed = []
    for g in range(KVH):
        keys = stage_gate_up[:, g * HD : (g + 1) * HD]
        values = stage_gate_up[:, (KVH + g) * HD : (KVH + g + 1) * HD]
        bias = jnp.concatenate([meta[s, g : g + 1, :] for s in range(N_SEQ)], axis=1)
        for pair in range(2):
            first = queries[g][:, pair * 2 * HD : (pair * 2 + 1) * HD]
            second = queries[g][:, (pair * 2 + 1) * HD : (pair * 2 + 2) * HD]
            both = attention_part(
                jnp.concatenate([first, second], axis=0), keys, values, bias, same
            )
            mixed.extend([both[0:TOK], both[TOK : 2 * TOK]])
        if g == 0:
            ring_2(2)
    ring_3(2)
    ring_4(2)
    mixed = jnp.concatenate(mixed, axis=1)
    projected = jnp.dot(
        mixed, down[...].reshape((OWN + 1) * HID, D), preferred_element_type=F32
    )
    residual_keep[...] = (tokens.astype(F32) + projected).astype(BF16)
    residual = residual_keep[...].astype(F32)
    inv_rms = lax.rsqrt(jnp.mean(residual * residual, axis=-1, keepdims=True) + 1e-05)
    moe_in = (residual * inv_rms * gain_ref[...]).astype(BF16)
    either = (places[0] + places[1]).astype(BF16)
    exchange_build(0, jnp.dot(either, moe_in, preferred_element_type=F32).astype(BF16))
    exchange_start(0)
    for which in range(4):
        ring_sent(which)
    load_start()
    for e in range(OWN):
        gather_4(1, e)
    exchange_end(0)
    gather_1(0, 0)
    gather_1(0, 1)
    gather_2(0, 0)
    gather_3(0, 0)
    gather_1(0, 2)
    gather_2(0, 1)
    gather_4(0, 0)
    gather_3(0, 1)
    for e in range(OWN):
        gather_5(1, e)
    gather_5(0, 0)
    compute(0)
    gather_4(0, 1)
    reduce_1(0)
    gather_2(0, 2)
    gather_3(0, 2)
    gather_5(0, 1)
    compute(1)
    gather_4(0, 2)
    reduce_2(0)
    reduce_1(1)
    gather_5(0, 2)
    compute(2)
    reduce_1(2)
    reduce_2(1)
    reduce_3(0)
    reduce_2(2)
    reduce_4(0)
    reduce_3(1)
    reduce_5(0)
    reduce_4(1)
    reduce_3(2)
    reduce_4(2)
    reduce_5(1)
    reduce_5(2)
    for copy in returned.values():
        copy.wait()
    for copy in reduces.values():
        copy.wait_send()
    for copy in stores[OWN - 1]:
        copy.wait()


def finish(ids, weights, back, residual, cot, gain, grads):
    vmem = pl.BlockSpec(memory_space=pltpu.VMEM)
    hbm = pl.BlockSpec(memory_space=pl.ANY)
    return pl.pallas_call(
        finish_kernel,
        out_shape=(
            jax.ShapeDtypeStruct((TOK, D), BF16),
            jax.ShapeDtypeStruct((TOK, D), BF16),
        )
        + tuple(jax.ShapeDtypeStruct(g.shape, BF16) for g in grads),
        in_specs=[vmem] * 6 + [hbm] * 3,
        out_specs=(vmem, vmem, hbm, hbm, hbm),
        scratch_shapes=[pltpu.SemaphoreType.DMA((OWN, 3))],
        compiler_params=pltpu.CompilerParams(vmem_limit_bytes=63 * 2**20),
        name="finish",
    )(ids, weights, back, residual, cot, gain, *grads)


def decoder_block(
    tokens, memory, bias, mem_session, session, cot, gain, ids, weights, projections, experts
):
    vmem = pl.BlockSpec(memory_space=pltpu.VMEM)
    hbm = pl.BlockSpec(memory_space=pl.ANY)
    corner = corner_matrix()
    dma = pltpu.SemaphoreType.DMA
    return pl.pallas_call(
        block_kernel,
        out_shape=(
            jax.ShapeDtypeStruct((N_SEQ, OWN * PACK, D), BF16),
            jax.ShapeDtypeStruct((TOK, D), BF16),
        )
        + tuple(jax.ShapeDtypeStruct(w.shape, BF16) for w in experts),
        in_specs=[vmem] * 12 + [hbm] * 7,
        out_specs=(vmem, vmem, hbm, hbm, hbm),
        scratch_shapes=[
            pltpu.VMEM((OWN, N_DP, BLK, D), BF16),
            pltpu.VMEM((OWN, D, 2 * HID), BF16),
            pltpu.VMEM((OWN + 1, HID, D), BF16),
            pltpu.VMEM((N_DP * SRC, HID), BF16),
            pltpu.VMEM((N_DP * SRC, 2 * HID), BF16),
            pltpu.VMEM((D, 2 * HID), BF16),
            pltpu.VMEM((MEM, D), BF16),
            pltpu.VMEM((N_SEQ, 8, MEM), F32),
            pltpu.VMEM((2, N_SEQ, 16, WIDE), BF16),
            pltpu.VMEM((2, N_SEQ, 16, WIDE), BF16),
            pltpu.VMEM((OWN, N_SEQ, PACK, D), BF16),
            pltpu.VMEM((OWN, 2, 4, BLK, HALF), BF16),
            pltpu.VMEM((OWN, 2, 2, 4, BLK, HALF), BF16),
            pltpu.VMEM((OWN, 2, 2, BLK, QUARTER), BF16),
            pltpu.VMEM((OWN, 2, 2, BLK, HALF), BF16),
            dma((5,)),
            dma((OWN, 3)),
            dma((OWN, 3)),
            dma((N_SEQ,)),
            dma((N_SEQ,)),
            dma((4, 8)),
            dma((4, 8)),
            dma((2, N_SEQ)),
            dma((2, N_SEQ)),
            dma((OWN, N_SEQ)),
            dma((OWN, N_SEQ)),
            dma((2, OWN, 2, 16)),
            dma((2, OWN, 2, 16)),
            dma((OWN, 2, 16)),
            dma((OWN, 2, 16)),
        ],
        compiler_params=pltpu.CompilerParams(
            collective_id=1, has_side_effects=True, vmem_limit_bytes=63 * 2**20
        ),
        name="decoder_block",
    )(
        tokens,
        bias,
        mem_session,
        session,
        cot,
        gain,
        ids,
        weights,
        jnp.asarray(compact_matrix(), BF16),
        jnp.asarray(corner, BF16),
        jnp.asarray(corner.T, BF16),
        jnp.asarray(return_matrix().T, BF16),
        memory,
        *projections,
        *experts,
    )


def per_device(
    tokens,
    memory,
    mem_session,
    dec_session,
    event_bias,
    expert_ids,
    route_weights,
    norm_gain,
    w_query,
    w_keyval,
    w_output,
    w_gate,
    w_up,
    w_down,
    cotangent,
):
    ids, weights = expert_ids[0].T, route_weights[0].T
    gain = norm_gain.reshape(1, D)
    back, residual, *grads = decoder_block(
        tokens[0],
        memory[0],
        event_bias[0],
        mem_session,
        dec_session,
        cotangent[0],
        gain,
        ids,
        weights,
        (w_query, w_keyval, w_output),
        (w_gate, w_up, w_down),
    )
    block_out, grad_resid, grad_gate, grad_up, grad_down = finish(
        ids, weights, back, residual, cotangent[0], gain, grads
    )
    return (block_out[None], grad_resid[None], grad_gate, grad_up, grad_down)


def solution(mesh):
    return jax.shard_map(
        per_device,
        mesh=mesh,
        in_specs=(
            P("dp", "seq", None),
            P("dp", "seq", None),
            P("dp", "seq"),
            P("dp", "seq"),
            P("dp", None, "seq"),
            P("dp", "seq", None),
            P("dp", "seq", None),
            P(),
            P("seq", None),
            P("seq", None),
            P("seq", None),
            P("seq", None, "dp"),
            P("seq", None, "dp"),
            P("seq", "dp", None),
            P("dp", "seq", None),
        ),
        out_specs=(
            P("dp", "seq", None),
            P("dp", "seq", None),
            P("seq", None, "dp"),
            P("seq", None, "dp"),
            P("seq", "dp", None),
        ),
        check_vma=False,
    )
```

```python
import functools

import jax
import jax.numpy as jnp
import numpy as np
from jax import lax
from jax.experimental import pallas as pl
from jax.experimental.pallas import tpu as pltpu
from jax.sharding import PartitionSpec as P

D = 2048
EXPERTS = 24
TOPK = 2
QH = 8
KVH = 2
HD = 128
CAP = 6
SIDE = 4
N_DP = 16
N_SEQ = 8
OWN = 3
HID = 256
TOK = 64
SRC = N_SEQ * CAP
BLK = 2 * SRC
PACK = 16
MEM = 256
WIDE = D + 256
KV = 2 * KVH * HD
HALF = D // 2
QUARTER = D // 4
MESH = pl.DeviceIdType.MESH
F32 = jnp.float32
BF16 = jnp.bfloat16
NT = (((1,), (1,)), ((), ()))
TN = (((0,), (0,)), ((), ()))


def return_matrix():
    table = np.zeros((BLK, N_SEQ * PACK), np.float32)
    for kind in range(2):
        for source in range(N_SEQ):
            for slot in range(CAP):
                table[kind * SRC + source * CAP + slot, source * PACK + kind * CAP + slot] = 1.0
    return table


def compact_matrix():
    table = np.zeros((OWN * SRC, OWN * SRC), np.float32)
    for expert in range(OWN):
        for source in range(N_SEQ):
            for slot in range(CAP):
                row = expert * CAP + slot
                column = source * 16 + row if row < 16 else N_SEQ * 16 + source * 2 + row - 16
                table[expert * SRC + source * CAP + slot, column] = 1.0
    return table


def corner_matrix():
    table = np.zeros((N_SEQ * 16, N_SEQ * 16), np.float32)
    for piece in range(8):
        for peer in range(N_SEQ):
            for last in range(2):
                table[peer * 16 + piece * 2 + last, piece * 16 + peer * 2 + last] = 1.0
    return table


def squares():
    down = lax.broadcasted_iota(jnp.int32, (TOK, TOK), 0)
    across = lax.broadcasted_iota(jnp.int32, (TOK, TOK), 1)
    return down, across


def as_column(row):
    down, across = squares()
    return jnp.sum(jnp.where(down == across, row, 0.0), axis=1, keepdims=True)


def one_hot(mask):
    return jnp.where(mask, 1.0, 0.0).astype(BF16)


def routed(ids_ref):
    down, across = squares()
    row = [ids_ref[k : k + 1, :].astype(F32) for k in range(TOPK)]
    column = [as_column(r) for r in row]

    def earlier(own, others, before, axis):
        named = sum(jnp.where(own == other, 1.0, 0.0) for other in others)
        return jnp.sum(jnp.where(before, named, 0.0), axis=axis, keepdims=True)

    row_slot = [earlier(row[k], column, down < across, 0) for k in range(TOPK)]
    column_slot = [earlier(column[k], row, across < down, 1) for k in range(TOPK)]
    return row, row_slot, column, column_slot


def send_places(ids_ref):
    row, row_slot, _, _ = routed(ids_ref)
    every = lax.broadcasted_iota(jnp.int32, (N_SEQ * 18, TOK), 0).astype(F32)
    places = []
    for k in range(TOPK):
        owner = jnp.floor((row[k] + 0.5) * (1.0 / OWN))
        place = (row[k] - OWN * owner) * CAP + row_slot[k]
        target = jnp.where(
            place < 16, owner * 16 + place, N_SEQ * 16 + owner * 2 + place - 16
        )
        places.append(jnp.where(every == target, 1.0, 0.0))
    return places


def add_rows(out, terms):
    @pl.loop(0, BLK // 16)
    def _(i):
        rows = pl.ds(pl.multiple_of(i * 16, 16), 16)
        total = terms[0][rows, :].astype(F32)
        for term in terms[1:]:
            total = total + term[rows, :].astype(F32)
        out[rows, :] = total.astype(BF16)


def finish_kernel(
    ids_ref,
    weight_ref,
    back_ref,
    residual_ref,
    cot_ref,
    gain_ref,
    gate_in,
    up_in,
    down_in,
    block_out_ref,
    grad_resid_ref,
    gate_out,
    up_out,
    down_out,
    gate_via,
    up_via,
    down_via,
    in_sem,
    out_sem,
):
    loads, copies = [], []
    for e in range(OWN):
        for i, (src, via, dst) in enumerate(
            ((gate_in, gate_via, gate_out), (up_in, up_via, up_out), (down_in, down_via, down_out))
        ):
            loads.append(pltpu.make_async_copy(src.at[e], via.at[e], in_sem.at[e, i]))
            copies.append(pltpu.make_async_copy(via.at[e], dst.at[e], out_sem.at[e, i]))
    for load in loads:
        load.start()
    for load, copy in zip(loads, copies):
        load.wait()
        copy.start()
    _, _, column, column_slot = routed(ids_ref)
    every = lax.broadcasted_iota(jnp.int32, (TOK, EXPERTS * PACK), 1).astype(F32)
    back = back_ref[...].reshape(EXPERTS * PACK, D)
    answers = [column[k] * PACK + column_slot[k] for k in range(TOPK)]
    residual = residual_ref[...].astype(F32)
    combined = None
    for k in range(TOPK):
        picked = jnp.dot(one_hot(every == answers[k]), back, preferred_element_type=F32)
        term = picked * as_column(weight_ref[k : k + 1, :])
        combined = term if combined is None else combined + term
    block_out_ref[...] = (residual + combined).astype(BF16)
    both = (every == answers[0] + CAP) | (every == answers[1] + CAP)
    grad_moe = jnp.dot(one_hot(both), back, preferred_element_type=F32)
    inv_rms = lax.rsqrt(jnp.mean(residual * residual, axis=-1, keepdims=True) + 1e-05)
    normed = residual * inv_rms
    grad_normed = grad_moe * gain_ref[...]
    correction = normed * jnp.mean(grad_normed * normed, axis=-1, keepdims=True)
    grad_resid_ref[...] = (
        cot_ref[...].astype(F32) + inv_rms * (grad_normed - correction)
    ).astype(BF16)
    for copy in copies:
        copy.wait()


def block_kernel(
    tokens_ref,
    bias_ref,
    mem_session_ref,
    session_ref,
    cot_ref,
    gain_ref,
    ids_ref,
    weight_ref,
    compact_ref,
    corner_ref,
    corner_back_ref,
    expand_ref,
    memory_hbm,
    query_hbm,
    keyval_hbm,
    output_hbm,
    gate_hbm,
    up_hbm,
    down_hbm,
    back_recv,
    residual_keep,
    grad_gate_hbm,
    grad_up_hbm,
    grad_down_hbm,
    rows,
    gate_up,
    down,
    hidden,
    grads,
    stage_gate_up,
    memory,
    meta,
    z_send,
    z_recv,
    back_send,
    first_far,
    first_near,
    second_far,
    second_near,
    own_sem,
    load_sem,
    store_sem,
    m_ssem,
    m_rsem,
    w_ssem,
    w_rsem,
    z_ssem,
    z_rsem,
    b_ssem,
    b_rsem,
    g_ssem,
    g_rsem,
    r_ssem,
    r_rsem,
):
    me = lax.axis_index("dp")
    seq = lax.axis_index("seq")
    mx, my = me // SIDE, me % SIDE
    mz, mc = seq // 2, seq % 2
    stage_down = down.at[OWN]

    def device(half, step1, step2):
        dx, dy = (step1, step2) if half == 0 else (step2, step1)
        return ((mx + dx + SIDE) % SIDE) * SIDE + (my + dy + SIDE) % SIDE

    def columns(half):
        return pl.ds(half * HALF, HALF)

    barrier = pltpu.get_barrier_semaphore()
    for half in range(2):
        for step in (1, -1):
            pl.semaphore_signal(
                barrier, inc=1, device_id=(device(half, step, 0), seq), device_id_type=MESH
            )
    for offset in range(1, N_SEQ):
        pl.semaphore_signal(
            barrier, inc=1, device_id=(me, (seq + offset) % N_SEQ), device_id_type=MESH
        )

    def remote(src, dst, ssem, rsem, target):
        copy = pltpu.make_async_remote_copy(
            src_ref=src,
            dst_ref=dst,
            send_sem=ssem,
            recv_sem=rsem,
            device_id=target,
            device_id_type=MESH,
        )
        copy.start()
        return copy

    own_rows = pl.ds(seq * MEM, MEM)
    own_loads = [
        pltpu.make_async_copy(keyval_hbm, gate_up.at[0, own_rows, :], own_sem.at[0]),
        pltpu.make_async_copy(query_hbm.at[:, pl.ds(0, KV)], gate_up.at[1, own_rows, :], own_sem.at[1]),
        pltpu.make_async_copy(query_hbm.at[:, pl.ds(KV, KV)], gate_up.at[2, own_rows, :], own_sem.at[2]),
        pltpu.make_async_copy(output_hbm, down.at[mz, pl.ds(mc * HD, HD), :], own_sem.at[3]),
        pltpu.make_async_copy(memory_hbm, memory, own_sem.at[4]),
    ]
    for copy in own_loads:
        copy.start()

    z_copies = {}

    def exchange_build(kind, packed):
        z_send[kind, :, :, 0:D] = packed[0 : N_SEQ * 16].reshape(N_SEQ, 16, D)
        last = packed[N_SEQ * 16 :]
        pieces = jnp.concatenate([last[:, i * 256 : (i + 1) * 256] for i in range(8)], axis=0)
        corner = jnp.dot(corner_ref[...], pieces, preferred_element_type=F32).astype(BF16)
        z_send[kind, :, :, D:WIDE] = corner.reshape(N_SEQ, 16, 256)

    def exchange_start(kind):
        for offset in range(1, N_SEQ):
            peer = (seq + offset) % N_SEQ
            z_copies[kind, offset] = remote(
                z_send.at[kind, peer],
                z_recv.at[kind, seq],
                z_ssem.at[kind, offset],
                z_rsem.at[kind, offset],
                (me, peer),
            )
        z_recv[kind, seq] = z_send[kind, seq]

    def exchange_end(kind):
        for offset in range(1, N_SEQ):
            z_copies[kind, offset].wait()
        first = z_recv[kind, :, :, 0:D].reshape(N_SEQ * 16, D)
        corner = z_recv[kind, :, :, D:WIDE].reshape(N_SEQ * 16, 256)
        pieces = jnp.dot(corner_back_ref[...], corner, preferred_element_type=F32).astype(BF16)
        last = jnp.concatenate([pieces[i * 16 : (i + 1) * 16] for i in range(8)], axis=1)
        arrived = jnp.concatenate([first, last], axis=0)
        compact = jnp.dot(compact_ref[...], arrived, preferred_element_type=F32).astype(BF16)
        for e in range(OWN):
            rows[e, me, kind * SRC : (kind + 1) * SRC, :] = compact[e * SRC : (e + 1) * SRC]

    ring = {}

    def keyval_weight_region(zz, cc, start, size):
        return gate_up.at[0, pl.ds((zz * 2 + cc) * MEM + start, size), :]

    def query_weight_region(zz, cc, start, size):
        return gate_up.at[pl.ds(1, 2), pl.ds((zz * 2 + cc) * MEM + start, size), :]

    def output_weight_region(zz, cc, start, size):
        return down.at[zz, pl.ds(cc * HD + start, size), :]

    def keyval_region(zz, cc, start, size):
        return stage_gate_up.at[pl.ds((zz * 2 + cc) * MEM + start, size), :]

    regions = [
        (keyval_weight_region, MEM),
        (query_weight_region, MEM),
        (output_weight_region, HD),
        (keyval_region, MEM),
    ]

    def ring_send(which, index, dz_owner, start, size, step, core):
        ref = regions[which][0]((mz + dz_owner + SIDE) % SIDE, mc, start, size)
        target = (me, ((mz + step + SIDE) % SIDE) * 2 + core)
        ring[which, index] = remote(ref, ref, w_ssem.at[which, index], w_rsem.at[which, index], target)

    def ring_1(which):
        size = regions[which][1]
        ring_send(which, 0, 0, 0, size, 1, mc)
        ring_send(which, 1, 0, 0, size, -1, mc)
        ring_send(which, 4, 0, 0, size, 0, 1 - mc)

    def ring_2(which):
        size = regions[which][1]
        ring[which, 0].wait_recv()
        ring_send(which, 2, -1, 0, size // 2, 1, mc)
        ring_send(which, 5, -1, 0, size, 0, 1 - mc)
        ring[which, 1].wait_recv()
        ring_send(which, 3, 1, size // 2, size // 2, -1, mc)
        ring_send(which, 6, 1, 0, size, 0, 1 - mc)

    def ring_3(which):
        ring[which, 2].wait_recv()
        ring[which, 3].wait_recv()
        ring_send(which, 7, 2, 0, regions[which][1], 0, 1 - mc)

    def ring_4(which):
        for index in range(4, 8):
            ring[which, index].wait_recv()

    def ring_sent(which):
        for index in range(8):
            ring[which, index].wait_send()

    def block(half, r1, r2):
        return device(half, r1, r2)

    gathers = {}

    def gather_send(kind, e, half, index, width, origin, steps):
        target = device(half, *steps)
        part = rows.at[e, origin, pl.ds(kind * SRC, SRC), width]
        copy = remote(part, part, g_ssem.at[kind, e, half, index], g_rsem.at[kind, e, half, index], (target, seq))
        gathers[kind, e, half, index] = copy

    def gather_1(kind, e):
        for half in range(2):
            cols = columns(half)
            gather_send(kind, e, half, 0, cols, me, (1, 0))
            gather_send(kind, e, half, 1, cols, me, (-1, 0))
        for half in range(2):
            cols = columns(half)
            gather_send(kind, e, half, 4, cols, me, (0, 1))
            gather_send(kind, e, half, 8, cols, me, (0, -1))

    def gather_2(kind, e):
        for half in range(2):
            cols = columns(half)
            gathers[kind, e, half, 0].wait_recv()
            gather_send(kind, e, half, 2, pl.ds(half * HALF, QUARTER), block(half, -1, 0), (1, 0))
            gathers[kind, e, half, 1].wait_recv()
            gather_send(kind, e, half, 3, pl.ds(half * HALF + QUARTER, QUARTER), block(half, 1, 0), (-1, 0))
            for r in (1, 3):
                gather_send(kind, e, half, 4 + r, cols, block(half, r, 0), (0, 1))
                gather_send(kind, e, half, 8 + r, cols, block(half, r, 0), (0, -1))

    def gather_3(kind, e):
        for half in range(2):
            cols = columns(half)
            gathers[kind, e, half, 2].wait_recv()
            gathers[kind, e, half, 3].wait_recv()
            gather_send(kind, e, half, 6, cols, block(half, 2, 0), (0, 1))
            gather_send(kind, e, half, 10, cols, block(half, 2, 0), (0, -1))

    def gather_4(kind, e):
        for r in (0, 1, 3, 2):
            for half in range(2):
                cols = columns(half)
                gathers[kind, e, half, 4 + r].wait_recv()
                gathers[kind, e, half, 8 + r].wait_recv()
                if r < 2:
                    gather_send(kind, e, half, 12 + r, cols, block(half, r, -1), (0, 1))
                else:
                    gather_send(kind, e, half, 12 + r, cols, block(half, r, 1), (0, -1))

    def gather_5(kind, e):
        for half in range(2):
            for r in range(4):
                gathers[kind, e, half, 12 + r].wait_recv()
            for index in range(16):
                gathers[kind, e, half, index].wait_send()

    loads = []

    def load_start():
        for e in range(OWN):
            loads.append(
                (
                    pltpu.make_async_copy(gate_hbm.at[e], gate_up.at[e, :, pl.ds(0, HID)], load_sem.at[e, 0]),
                    pltpu.make_async_copy(up_hbm.at[e], gate_up.at[e, :, pl.ds(HID, HID)], load_sem.at[e, 1]),
                    pltpu.make_async_copy(down_hbm.at[e], down.at[e], load_sem.at[e, 2]),
                )
            )
        for group in loads:
            for copy in group:
                copy.start()

    stores = {}

    def compute(e):
        for copy in loads[e]:
            copy.wait()
        if e > 0:
            for copy in stores[e - 1]:
                copy.wait()
        group = 8
        tile = group * SRC

        @pl.loop(0, N_DP // group)
        def _(j):
            blocks = pl.ds(j * group, group)
            out_rows = pl.ds(pl.multiple_of(j * tile, tile), tile)
            inputs = rows[e, blocks, 0:SRC, :].reshape(tile, D)
            both = jnp.dot(inputs, gate_up[e], preferred_element_type=F32)
            outer = rows[e, blocks, SRC:BLK, :].reshape(tile, D)
            grad_hidden = lax.dot_general(outer, down[e], NT, preferred_element_type=F32)
            gate_pre, up_value = both[:, :HID], both[:, HID:]
            sigmoid = jax.nn.sigmoid(gate_pre)
            activated = gate_pre * sigmoid
            hidden[out_rows, :] = (activated * up_value).astype(BF16)
            grads[out_rows, 0:HID] = (
                grad_hidden * up_value * sigmoid * (1.0 + gate_pre * (1.0 - sigmoid))
            ).astype(BF16)
            grads[out_rows, HID : 2 * HID] = (grad_hidden * activated).astype(BF16)

        @pl.loop(0, D // 256)
        def _(j):
            cols = pl.ds(pl.multiple_of(j * 256, 256), 256)
            inputs = rows[e, :, 0:SRC, cols].reshape(N_DP * SRC, 256)
            stage_gate_up[cols, :] = lax.dot_general(
                inputs, grads[...], TN, preferred_element_type=F32
            ).astype(BF16)
            outer = rows[e, :, SRC:BLK, cols].reshape(N_DP * SRC, 256)
            down[OWN, :, cols] = lax.dot_general(
                hidden[...], outer, TN, preferred_element_type=F32
            ).astype(BF16)

        stores[e] = (
            pltpu.make_async_copy(stage_gate_up.at[:, pl.ds(0, HID)], grad_gate_hbm.at[e], store_sem.at[e, 0]),
            pltpu.make_async_copy(stage_gate_up.at[:, pl.ds(HID, HID)], grad_up_hbm.at[e], store_sem.at[e, 1]),
            pltpu.make_async_copy(stage_down, grad_down_hbm.at[e], store_sem.at[e, 2]),
        )
        for copy in stores[e]:
            copy.start()

        @pl.loop(0, D // 256)
        def _(j):
            cols = pl.ds(pl.multiple_of(j * 256, 256), 256)
            out = jnp.dot(hidden[...], down[e, :, cols], preferred_element_type=F32)
            rows[e, :, 0:SRC, cols] = out.astype(BF16).reshape(N_DP, SRC, 256)
            back = lax.dot_general(grads[...], gate_up[e, cols, :], NT, preferred_element_type=F32)
            rows[e, :, SRC:BLK, cols] = back.astype(BF16).reshape(N_DP, SRC, 256)

    reduces = {}

    def reduce_send(e, half, index, src, dst, steps):
        target = device(half, *steps)
        copy = remote(src, dst, r_ssem.at[e, half, index], r_rsem.at[e, half, index], (target, seq))
        reduces[e, half, index] = copy

    def part(e, half, r1, r2):
        return rows.at[e, block(half, r1, r2), :, columns(half)]

    def reduce_1(e):
        for half in range(2):
            for r in range(4):
                step = 1 if r < 2 else -1
                reduce_send(e, half, r, part(e, half, r, 2), first_far.at[e, half, r], (0, step))
        for half in range(2):
            for r in (2, 3):
                reduce_send(e, half, 4 + r, part(e, half, r, 1), first_near.at[e, half, 0, r], (0, 1))
            for r in (0, 1):
                reduce_send(e, half, 8 + r, part(e, half, r, -1), first_near.at[e, half, 1, r], (0, -1))

    def reduce_2(e):
        for r in range(4):
            for half in range(2):
                step = 1 if r < 2 else -1
                reduces[e, half, r].wait_recv()
                mine = part(e, half, r, step)
                add_rows(mine, [mine, first_far.at[e, half, r]])
                way = 0 if r < 2 else 1
                reduce_send(
                    e, half, 4 + 4 * way + r, mine, first_near.at[e, half, way, r], (0, step)
                )

    def reduce_3(e):
        for r in (2, 1, 3, 0):
            for half in range(2):
                reduces[e, half, 4 + r].wait_recv()
                reduces[e, half, 8 + r].wait_recv()
                mine = part(e, half, r, 0)
                add_rows(
                    mine, [mine, first_near.at[e, half, 0, r], first_near.at[e, half, 1, r]]
                )
                if r == 2:
                    for way, step in ((0, 1), (1, -1)):
                        quarter = pl.ds(half * HALF + way * QUARTER, QUARTER)
                        src = rows.at[e, block(half, 2, 0), :, quarter]
                        reduce_send(e, half, 12 + way, src, second_far.at[e, half, way], (step, 0))

    def reduce_4(e):
        for half in range(2):
            for way, step in ((0, 1), (1, -1)):
                reduces[e, half, 12 + way].wait_recv()
                quarter = pl.ds(half * HALF + way * QUARTER, QUARTER)
                mine = rows.at[e, block(half, step, 0), :, quarter]
                add_rows(mine, [mine, second_far.at[e, half, way]])
                reduce_send(
                    e, half, 14 + way, part(e, half, step, 0), second_near.at[e, half, way], (step, 0)
                )

    returned = {}

    def reduce_5(e):
        for half in range(2):
            for way in range(2):
                reduces[e, half, 14 + way].wait_recv()
            mine = part(e, half, 0, 0)
            add_rows(mine, [mine, second_near.at[e, half, 0], second_near.at[e, half, 1]])
        back_send[e] = (
            jnp.dot(expand_ref[...], rows[e, me], preferred_element_type=F32)
            .astype(BF16)
            .reshape(N_SEQ, PACK, D)
        )
        for offset in range(1, N_SEQ):
            peer = (seq + offset) % N_SEQ
            returned[e, offset] = remote(
                back_send.at[e, peer],
                back_recv.at[seq, pl.ds(e * PACK, PACK)],
                b_ssem.at[e, offset],
                b_rsem.at[e, offset],
                (me, peer),
            )
        back_recv[seq, e * PACK : (e + 1) * PACK, :] = back_send[e, seq]

    def attention_part(queries, keys, values, bias, same):
        scores = lax.dot_general(queries, keys, NT, preferred_element_type=F32) * HD ** (-0.5)
        scores = jnp.where(same, scores + bias, -1e30)
        row_max = jnp.max(scores, axis=-1, keepdims=True)
        raised = jnp.exp(scores - row_max)
        probability = (raised / jnp.sum(raised, axis=-1, keepdims=True)).astype(BF16)
        return jnp.dot(probability, values, preferred_element_type=F32).astype(BF16)

    places = send_places(ids_ref)
    cot = cot_ref[...].astype(F32)
    packed = None
    for k in range(TOPK):
        grad_out = (as_column(weight_ref[k : k + 1, :]) * cot).astype(BF16)
        term = jnp.dot(places[k].astype(BF16), grad_out, preferred_element_type=F32)
        packed = term if packed is None else packed + term
    exchange_build(1, packed.astype(BF16))
    meta[seq] = jnp.concatenate(
        [bias_ref[...], mem_session_ref[...].astype(F32), jnp.zeros((8 - KVH - 1, MEM), F32)],
        axis=0,
    )
    own_loads[0].wait()
    pl.semaphore_wait(barrier, 4 + N_SEQ - 1)

    exchange_start(1)
    meta_copies = []
    for offset in range(1, N_SEQ):
        peer = (seq + offset) % N_SEQ
        meta_copies.append(
            remote(meta.at[seq], meta.at[seq], m_ssem.at[offset], m_rsem.at[offset], (me, peer))
        )
    ring_1(0)
    for copy in own_loads[1:]:
        copy.wait()
    ring_2(0)
    ring_1(1)
    exchange_end(1)
    for e in range(OWN):
        gather_1(1, e)
    ring_3(0)
    ring_4(0)
    stage_gate_up[own_rows, :] = jnp.dot(
        memory[...], gate_up[0], preferred_element_type=F32
    ).astype(BF16)
    ring_1(3)
    ring_2(1)
    for e in range(OWN):
        gather_2(1, e)
    ring_2(3)
    ring_1(2)
    ring_3(1)
    for e in range(OWN):
        gather_3(1, e)
    ring_3(3)
    ring_4(1)
    tokens = tokens_ref[...]
    queries = [
        jnp.dot(tokens, gate_up[1 + g], preferred_element_type=F32).astype(BF16) for g in range(KVH)
    ]
    for copy in meta_copies:
        copy.wait()
    ring_4(3)
    session_all = jnp.concatenate([meta[s, 2:3, :] for s in range(N_SEQ)], axis=1)
    own_session = as_column(session_ref[...].astype(F32))
    same = jnp.concatenate([own_session, own_session], axis=0) == session_all
    mixed = []
    for g in range(KVH):
        keys = stage_gate_up[:, g * HD : (g + 1) * HD]
        values = stage_gate_up[:, (KVH + g) * HD : (KVH + g + 1) * HD]
        bias = jnp.concatenate([meta[s, g : g + 1, :] for s in range(N_SEQ)], axis=1)
        for pair in range(2):
            first = queries[g][:, pair * 2 * HD : (pair * 2 + 1) * HD]
            second = queries[g][:, (pair * 2 + 1) * HD : (pair * 2 + 2) * HD]
            both = attention_part(
                jnp.concatenate([first, second], axis=0), keys, values, bias, same
            )
            mixed.extend([both[0:TOK], both[TOK : 2 * TOK]])
        if g == 0:
            ring_2(2)
    ring_3(2)
    ring_4(2)
    mixed = jnp.concatenate(mixed, axis=1)
    projected = jnp.dot(
        mixed, down[...].reshape((OWN + 1) * HID, D), preferred_element_type=F32
    )
    residual_keep[...] = (tokens.astype(F32) + projected).astype(BF16)
    residual = residual_keep[...].astype(F32)
    inv_rms = lax.rsqrt(jnp.mean(residual * residual, axis=-1, keepdims=True) + 1e-05)
    moe_in = (residual * inv_rms * gain_ref[...]).astype(BF16)
    either = (places[0] + places[1]).astype(BF16)
    exchange_build(0, jnp.dot(either, moe_in, preferred_element_type=F32).astype(BF16))
    exchange_start(0)
    for which in range(4):
        ring_sent(which)
    load_start()
    for e in range(OWN):
        gather_4(1, e)
    exchange_end(0)
    gather_1(0, 0)
    gather_1(0, 1)
    gather_1(0, 2)
    gather_2(0, 0)
    gather_2(0, 1)
    gather_2(0, 2)
    gather_3(0, 0)
    gather_3(0, 1)
    gather_3(0, 2)
    for e in range(OWN):
        gather_5(1, e)
    gather_4(0, 0)
    gather_4(0, 1)
    gather_4(0, 2)
    gather_5(0, 0)
    compute(0)
    reduce_1(0)
    gather_5(0, 1)
    compute(1)
    reduce_2(0)
    reduce_1(1)
    gather_5(0, 2)
    compute(2)
    reduce_1(2)
    reduce_2(1)
    reduce_3(0)
    reduce_2(2)
    reduce_4(0)
    reduce_3(1)
    reduce_5(0)
    reduce_4(1)
    reduce_3(2)
    reduce_4(2)
    reduce_5(1)
    reduce_5(2)
    for copy in returned.values():
        copy.wait()
    for copy in reduces.values():
        copy.wait_send()
    for copy in stores[OWN - 1]:
        copy.wait()


def finish(ids, weights, back, residual, cot, gain, grads):
    vmem = pl.BlockSpec(memory_space=pltpu.VMEM)
    hbm = pl.BlockSpec(memory_space=pl.ANY)
    return pl.pallas_call(
        finish_kernel,
        out_shape=(
            jax.ShapeDtypeStruct((TOK, D), BF16),
            jax.ShapeDtypeStruct((TOK, D), BF16),
        )
        + tuple(jax.ShapeDtypeStruct(g.shape, BF16) for g in grads),
        in_specs=[vmem] * 6 + [hbm] * 3,
        out_specs=(vmem, vmem, hbm, hbm, hbm),
        scratch_shapes=[pltpu.VMEM(g.shape, BF16) for g in grads]
        + [pltpu.SemaphoreType.DMA((OWN, 3)), pltpu.SemaphoreType.DMA((OWN, 3))],
        compiler_params=pltpu.CompilerParams(vmem_limit_bytes=63 * 2**20),
        name="finish",
    )(ids, weights, back, residual, cot, gain, *grads)


def decoder_block(
    tokens, memory, bias, mem_session, session, cot, gain, ids, weights, projections, experts
):
    vmem = pl.BlockSpec(memory_space=pltpu.VMEM)
    hbm = pl.BlockSpec(memory_space=pl.ANY)
    corner = corner_matrix()
    dma = pltpu.SemaphoreType.DMA
    return pl.pallas_call(
        block_kernel,
        out_shape=(
            jax.ShapeDtypeStruct((N_SEQ, OWN * PACK, D), BF16),
            jax.ShapeDtypeStruct((TOK, D), BF16),
        )
        + tuple(jax.ShapeDtypeStruct(w.shape, BF16) for w in experts),
        in_specs=[vmem] * 12 + [hbm] * 7,
        out_specs=(vmem, vmem, hbm, hbm, hbm),
        scratch_shapes=[
            pltpu.VMEM((OWN, N_DP, BLK, D), BF16),
            pltpu.VMEM((OWN, D, 2 * HID), BF16),
            pltpu.VMEM((OWN + 1, HID, D), BF16),
            pltpu.VMEM((N_DP * SRC, HID), BF16),
            pltpu.VMEM((N_DP * SRC, 2 * HID), BF16),
            pltpu.VMEM((D, 2 * HID), BF16),
            pltpu.VMEM((MEM, D), BF16),
            pltpu.VMEM((N_SEQ, 8, MEM), F32),
            pltpu.VMEM((2, N_SEQ, 16, WIDE), BF16),
            pltpu.VMEM((2, N_SEQ, 16, WIDE), BF16),
            pltpu.VMEM((OWN, N_SEQ, PACK, D), BF16),
            pltpu.VMEM((OWN, 2, 4, BLK, HALF), BF16),
            pltpu.VMEM((OWN, 2, 2, 4, BLK, HALF), BF16),
            pltpu.VMEM((OWN, 2, 2, BLK, QUARTER), BF16),
            pltpu.VMEM((OWN, 2, 2, BLK, HALF), BF16),
            dma((5,)),
            dma((OWN, 3)),
            dma((OWN, 3)),
            dma((N_SEQ,)),
            dma((N_SEQ,)),
            dma((4, 8)),
            dma((4, 8)),
            dma((2, N_SEQ)),
            dma((2, N_SEQ)),
            dma((OWN, N_SEQ)),
            dma((OWN, N_SEQ)),
            dma((2, OWN, 2, 16)),
            dma((2, OWN, 2, 16)),
            dma((OWN, 2, 16)),
            dma((OWN, 2, 16)),
        ],
        compiler_params=pltpu.CompilerParams(
            collective_id=1, has_side_effects=True, vmem_limit_bytes=63 * 2**20
        ),
        name="decoder_block",
    )(
        tokens,
        bias,
        mem_session,
        session,
        cot,
        gain,
        ids,
        weights,
        jnp.asarray(compact_matrix(), BF16),
        jnp.asarray(corner, BF16),
        jnp.asarray(corner.T, BF16),
        jnp.asarray(return_matrix().T, BF16),
        memory,
        *projections,
        *experts,
    )


def per_device(
    tokens,
    memory,
    mem_session,
    dec_session,
    event_bias,
    expert_ids,
    route_weights,
    norm_gain,
    w_query,
    w_keyval,
    w_output,
    w_gate,
    w_up,
    w_down,
    cotangent,
):
    ids, weights = expert_ids[0].T, route_weights[0].T
    gain = norm_gain.reshape(1, D)
    back, residual, *grads = decoder_block(
        tokens[0],
        memory[0],
        event_bias[0],
        mem_session,
        dec_session,
        cotangent[0],
        gain,
        ids,
        weights,
        (w_query, w_keyval, w_output),
        (w_gate, w_up, w_down),
    )
    block_out, grad_resid, grad_gate, grad_up, grad_down = finish(
        ids, weights, back, residual, cotangent[0], gain, grads
    )
    return (block_out[None], grad_resid[None], grad_gate, grad_up, grad_down)


def solution(mesh):
    return jax.shard_map(
        per_device,
        mesh=mesh,
        in_specs=(
            P("dp", "seq", None),
            P("dp", "seq", None),
            P("dp", "seq"),
            P("dp", "seq"),
            P("dp", None, "seq"),
            P("dp", "seq", None),
            P("dp", "seq", None),
            P(),
            P("seq", None),
            P("seq", None),
            P("seq", None),
            P("seq", None, "dp"),
            P("seq", None, "dp"),
            P("seq", "dp", None),
            P("dp", "seq", None),
        ),
        out_specs=(
            P("dp", "seq", None),
            P("dp", "seq", None),
            P("seq", None, "dp"),
            P("seq", None, "dp"),
            P("seq", "dp", None),
        ),
        check_vma=False,
    )
```

```python
import functools

import jax
import jax.numpy as jnp
import numpy as np
from jax import lax
from jax.experimental import pallas as pl
from jax.experimental.pallas import tpu as pltpu
from jax.sharding import PartitionSpec as P

D = 2048
EXPERTS = 24
TOPK = 2
QH = 8
KVH = 2
HD = 128
CAP = 6
SIDE = 4
N_DP = 16
N_SEQ = 8
OWN = 3
HID = 256
TOK = 64
SRC = N_SEQ * CAP
BLK = 2 * SRC
PACK = 16
MEM = 256
WIDE = D + 256
KV = 2 * KVH * HD
STRIP = HD // 4
HALF = D // 2
QUARTER = D // 4
MESH = pl.DeviceIdType.MESH
F32 = jnp.float32
BF16 = jnp.bfloat16
NT = (((1,), (1,)), ((), ()))
TN = (((0,), (0,)), ((), ()))


def return_matrix():
    table = np.zeros((BLK, N_SEQ * PACK), np.float32)
    for kind in range(2):
        for source in range(N_SEQ):
            for slot in range(CAP):
                table[kind * SRC + source * CAP + slot, source * PACK + kind * CAP + slot] = 1.0
    return table


def compact_matrix():
    table = np.zeros((OWN * SRC, OWN * SRC), np.float32)
    for expert in range(OWN):
        for source in range(N_SEQ):
            for slot in range(CAP):
                row = expert * CAP + slot
                column = source * 16 + row if row < 16 else N_SEQ * 16 + source * 2 + row - 16
                table[expert * SRC + source * CAP + slot, column] = 1.0
    return table


def corner_matrix():
    table = np.zeros((N_SEQ * 16, N_SEQ * 16), np.float32)
    for piece in range(8):
        for peer in range(N_SEQ):
            for last in range(2):
                table[peer * 16 + piece * 2 + last, piece * 16 + peer * 2 + last] = 1.0
    return table


def squares():
    down = lax.broadcasted_iota(jnp.int32, (TOK, TOK), 0)
    across = lax.broadcasted_iota(jnp.int32, (TOK, TOK), 1)
    return down, across


def as_column(row):
    down, across = squares()
    return jnp.sum(jnp.where(down == across, row, 0.0), axis=1, keepdims=True)


def one_hot(mask):
    return jnp.where(mask, 1.0, 0.0).astype(BF16)


def routed(ids_ref):
    down, across = squares()
    row = [ids_ref[k : k + 1, :].astype(F32) for k in range(TOPK)]
    column = [as_column(r) for r in row]

    def earlier(own, others, before, axis):
        named = sum(jnp.where(own == other, 1.0, 0.0) for other in others)
        return jnp.sum(jnp.where(before, named, 0.0), axis=axis, keepdims=True)

    row_slot = [earlier(row[k], column, down < across, 0) for k in range(TOPK)]
    column_slot = [earlier(column[k], row, across < down, 1) for k in range(TOPK)]
    return row, row_slot, column, column_slot


def send_places(ids_ref):
    row, row_slot, _, _ = routed(ids_ref)
    every = lax.broadcasted_iota(jnp.int32, (N_SEQ * 18, TOK), 0).astype(F32)
    places = []
    for k in range(TOPK):
        owner = jnp.floor((row[k] + 0.5) * (1.0 / OWN))
        place = (row[k] - OWN * owner) * CAP + row_slot[k]
        target = jnp.where(
            place < 16, owner * 16 + place, N_SEQ * 16 + owner * 2 + place - 16
        )
        places.append(jnp.where(every == target, 1.0, 0.0))
    return places


def add_rows(out, terms):
    @pl.loop(0, BLK // 16)
    def _(i):
        rows = pl.ds(pl.multiple_of(i * 16, 16), 16)
        total = terms[0][rows, :].astype(F32)
        for term in terms[1:]:
            total = total + term[rows, :].astype(F32)
        out[rows, :] = total.astype(BF16)


def finish_kernel(
    ids_ref,
    weight_ref,
    back_ref,
    residual_ref,
    cot_ref,
    gain_ref,
    gate_in,
    up_in,
    down_in,
    block_out_ref,
    grad_resid_ref,
    gate_out,
    up_out,
    down_out,
    gate_via,
    up_via,
    down_via,
    in_sem,
    out_sem,
):
    loads, copies = [], []
    for e in range(OWN):
        for i, (src, via, dst) in enumerate(
            ((gate_in, gate_via, gate_out), (up_in, up_via, up_out), (down_in, down_via, down_out))
        ):
            loads.append(pltpu.make_async_copy(src.at[e], via.at[e], in_sem.at[e, i]))
            copies.append(pltpu.make_async_copy(via.at[e], dst.at[e], out_sem.at[e, i]))
    for load in loads:
        load.start()
    _, _, column, column_slot = routed(ids_ref)
    every = lax.broadcasted_iota(jnp.int32, (TOK, EXPERTS * PACK), 1).astype(F32)
    back = back_ref[...].reshape(EXPERTS * PACK, D)
    answers = [column[k] * PACK + column_slot[k] for k in range(TOPK)]
    residual = residual_ref[...].astype(F32)
    combined = None
    for k in range(TOPK):
        picked = jnp.dot(one_hot(every == answers[k]), back, preferred_element_type=F32)
        term = picked * as_column(weight_ref[k : k + 1, :])
        combined = term if combined is None else combined + term
    block_out_ref[...] = (residual + combined).astype(BF16)
    both = (every == answers[0] + CAP) | (every == answers[1] + CAP)
    grad_moe = jnp.dot(one_hot(both), back, preferred_element_type=F32)
    inv_rms = lax.rsqrt(jnp.mean(residual * residual, axis=-1, keepdims=True) + 1e-05)
    normed = residual * inv_rms
    grad_normed = grad_moe * gain_ref[...]
    correction = normed * jnp.mean(grad_normed * normed, axis=-1, keepdims=True)
    grad_resid_ref[...] = (
        cot_ref[...].astype(F32) + inv_rms * (grad_normed - correction)
    ).astype(BF16)
    for load, copy in zip(loads, copies):
        load.wait()
        copy.start()
    for copy in copies:
        copy.wait()


def block_kernel(
    tokens_ref,
    bias_ref,
    mem_session_ref,
    session_ref,
    cot_ref,
    gain_ref,
    ids_ref,
    weight_ref,
    compact_ref,
    corner_ref,
    corner_back_ref,
    expand_ref,
    memory_hbm,
    query_hbm,
    keyval_hbm,
    output_hbm,
    gate_hbm,
    up_hbm,
    down_hbm,
    back_recv,
    residual_keep,
    grad_gate_hbm,
    grad_up_hbm,
    grad_down_hbm,
    rows,
    gate_up,
    down,
    hidden,
    grads,
    stage_gate_up,
    memory,
    meta,
    z_send,
    z_recv,
    back_send,
    first_far,
    first_near,
    second_far,
    second_near,
    own_sem,
    load_sem,
    store_sem,
    m_ssem,
    m_rsem,
    s_ssem,
    s_rsem,
    w_ssem,
    w_rsem,
    z_ssem,
    z_rsem,
    b_ssem,
    b_rsem,
    g_ssem,
    g_rsem,
    r_ssem,
    r_rsem,
):
    me = lax.axis_index("dp")
    seq = lax.axis_index("seq")
    mx, my = me // SIDE, me % SIDE
    mz, mc = seq // 2, seq % 2
    stage_down = down.at[OWN]

    def device(half, step1, step2):
        dx, dy = (step1, step2) if half == 0 else (step2, step1)
        return ((mx + dx + SIDE) % SIDE) * SIDE + (my + dy + SIDE) % SIDE

    def columns(half):
        return pl.ds(half * HALF, HALF)

    barrier = pltpu.get_barrier_semaphore()
    for half in range(2):
        for step in (1, -1, 2):
            pl.semaphore_signal(
                barrier, inc=1, device_id=(device(half, step, 0), seq), device_id_type=MESH
            )
    for offset in range(1, N_SEQ):
        pl.semaphore_signal(
            barrier, inc=1, device_id=(me, (seq + offset) % N_SEQ), device_id_type=MESH
        )

    def remote(src, dst, ssem, rsem, target):
        copy = pltpu.make_async_remote_copy(
            src_ref=src,
            dst_ref=dst,
            send_sem=ssem,
            recv_sem=rsem,
            device_id=target,
            device_id_type=MESH,
        )
        copy.start()
        return copy

    own_rows = pl.ds(seq * MEM, MEM)
    own_loads = [
        pltpu.make_async_copy(keyval_hbm, gate_up.at[0, own_rows, :], own_sem.at[0]),
        pltpu.make_async_copy(query_hbm.at[:, pl.ds(0, KV)], gate_up.at[1, own_rows, :], own_sem.at[1]),
        pltpu.make_async_copy(query_hbm.at[:, pl.ds(KV, KV)], gate_up.at[2, own_rows, :], own_sem.at[2]),
        pltpu.make_async_copy(output_hbm, down.at[mz, pl.ds(mc * HD, HD), :], own_sem.at[3]),
        pltpu.make_async_copy(memory_hbm, memory, own_sem.at[4]),
    ]
    for copy in own_loads:
        copy.start()

    z_copies = {}

    def exchange_build(kind, packed):
        z_send[kind, :, :, 0:D] = packed[0 : N_SEQ * 16].reshape(N_SEQ, 16, D)
        last = packed[N_SEQ * 16 :]
        pieces = jnp.concatenate([last[:, i * 256 : (i + 1) * 256] for i in range(8)], axis=0)
        corner = jnp.dot(corner_ref[...], pieces, preferred_element_type=F32).astype(BF16)
        z_send[kind, :, :, D:WIDE] = corner.reshape(N_SEQ, 16, 256)

    def exchange_start(kind):
        for offset in range(1, N_SEQ):
            peer = (seq + offset) % N_SEQ
            z_copies[kind, offset] = remote(
                z_send.at[kind, peer],
                z_recv.at[kind, seq],
                z_ssem.at[kind, offset],
                z_rsem.at[kind, offset],
                (me, peer),
            )
        z_recv[kind, seq] = z_send[kind, seq]

    def exchange_end(kind):
        for offset in range(1, N_SEQ):
            z_copies[kind, offset].wait()
        first = z_recv[kind, :, :, 0:D].reshape(N_SEQ * 16, D)
        corner = z_recv[kind, :, :, D:WIDE].reshape(N_SEQ * 16, 256)
        pieces = jnp.dot(corner_back_ref[...], corner, preferred_element_type=F32).astype(BF16)
        last = jnp.concatenate([pieces[i * 16 : (i + 1) * 16] for i in range(8)], axis=1)
        arrived = jnp.concatenate([first, last], axis=0)
        compact = jnp.dot(compact_ref[...], arrived, preferred_element_type=F32).astype(BF16)
        for e in range(OWN):
            rows[e, me, kind * SRC : (kind + 1) * SRC, :] = compact[e * SRC : (e + 1) * SRC]

    ring = {}

    def keyval_weight_region(zz, cc, start, size):
        return gate_up.at[0, pl.ds((zz * 2 + cc) * MEM + start, size), :]

    def query_weight_region(zz, cc, start, size):
        return gate_up.at[pl.ds(1, 2), pl.ds((zz * 2 + cc) * MEM + start, size), :]

    def keyval_region(zz, cc, start, size):
        return stage_gate_up.at[pl.ds((zz * 2 + cc) * MEM + start, size), :]

    regions = [
        (keyval_weight_region, MEM),
        (query_weight_region, MEM),
        None,
        (keyval_region, MEM),
    ]

    def ring_send(which, index, dz_owner, start, size, step, core):
        ref = regions[which][0]((mz + dz_owner + SIDE) % SIDE, mc, start, size)
        target = (me, ((mz + step + SIDE) % SIDE) * 2 + core)
        ring[which, index] = remote(ref, ref, w_ssem.at[which, index], w_rsem.at[which, index], target)

    def ring_1(which):
        size = regions[which][1]
        ring_send(which, 0, 0, 0, size, 1, mc)
        ring_send(which, 1, 0, 0, size, -1, mc)
        ring_send(which, 4, 0, 0, size, 0, 1 - mc)

    def ring_2(which):
        size = regions[which][1]
        ring[which, 0].wait_recv()
        ring_send(which, 2, -1, 0, size // 2, 1, mc)
        ring_send(which, 5, -1, 0, size, 0, 1 - mc)
        ring[which, 1].wait_recv()
        ring_send(which, 3, 1, size // 2, size // 2, -1, mc)
        ring_send(which, 6, 1, 0, size, 0, 1 - mc)

    def ring_3(which):
        ring[which, 2].wait_recv()
        ring[which, 3].wait_recv()
        ring_send(which, 7, 2, 0, regions[which][1], 0, 1 - mc)

    def ring_4(which):
        for index in range(4, 8):
            ring[which, index].wait_recv()

    def ring_sent(which):
        for index in range(8):
            ring[which, index].wait_send()

    spread = {}
    others = (-1, 1, 2)

    def quarter_of(dz_owner, half, start, size):
        place = mc * HD + (mx if half == 0 else my) * STRIP + start
        return down.at[(mz + dz_owner + SIDE) % SIDE, pl.ds(place, size), columns(half)]

    def strip_send(half, index, dz_owner, start, size, step):
        ref = quarter_of(dz_owner, half, start, size)
        which = 2 + 2 * half
        target = (me, ((mz + step + SIDE) % SIDE) * 2 + mc)
        ring[which, index] = remote(ref, ref, w_ssem.at[which, index], w_rsem.at[which, index], target)

    def shard_to_sibling(index, dz_owner):
        ref = down.at[(mz + dz_owner + SIDE) % SIDE, pl.ds(mc * HD, HD), :]
        ring[2, index] = remote(
            ref, ref, w_ssem.at[2, index], w_rsem.at[2, index], (me, mz * 2 + 1 - mc)
        )

    def strip_spread(half, other):
        ref = quarter_of(others[other], half, 0, STRIP)
        for peer in range(3):
            spread[half, other, peer] = remote(
                ref,
                ref,
                s_ssem.at[half, other, peer],
                s_rsem.at[half, other, peer],
                (device(half, others[peer], 0), seq),
            )

    def output_1():
        for half in range(2):
            strip_send(half, 0, 0, 0, STRIP, 1)
            strip_send(half, 1, 0, 0, STRIP, -1)
        shard_to_sibling(4, 0)

    def output_2():
        for half in range(2):
            ring[2 + 2 * half, 0].wait_recv()
            strip_send(half, 2, -1, 0, STRIP // 2, 1)
            strip_spread(half, 0)
            ring[2 + 2 * half, 1].wait_recv()
            strip_send(half, 3, 1, STRIP // 2, STRIP // 2, -1)
            strip_spread(half, 1)

    def output_3():
        for half in range(2):
            ring[2 + 2 * half, 2].wait_recv()
            ring[2 + 2 * half, 3].wait_recv()
            strip_spread(half, 2)

    def output_4():
        for other in range(3):
            for half in range(2):
                for peer in range(3):
                    spread[half, other, peer].wait_recv()
            shard_to_sibling(5 + other, others[other])

    def output_5():
        for index in range(4, 8):
            ring[2, index].wait_recv()

    def output_sent():
        for copy in spread.values():
            copy.wait_send()
        for index in range(4):
            ring[4, index].wait_send()

    def block(half, r1, r2):
        return device(half, r1, r2)

    gathers = {}

    def gather_send(kind, e, half, index, width, origin, steps):
        target = device(half, *steps)
        part = rows.at[e, origin, pl.ds(kind * SRC, SRC), width]
        copy = remote(part, part, g_ssem.at[kind, e, half, index], g_rsem.at[kind, e, half, index], (target, seq))
        gathers[kind, e, half, index] = copy

    def gather_1(kind, e):
        for half in range(2):
            cols = columns(half)
            gather_send(kind, e, half, 0, cols, me, (1, 0))
            gather_send(kind, e, half, 1, cols, me, (-1, 0))
        for half in range(2):
            cols = columns(half)
            gather_send(kind, e, half, 4, cols, me, (0, 1))
            gather_send(kind, e, half, 8, cols, me, (0, -1))

    def gather_2(kind, e):
        for half in range(2):
            cols = columns(half)
            gathers[kind, e, half, 0].wait_recv()
            gather_send(kind, e, half, 2, pl.ds(half * HALF, QUARTER), block(half, -1, 0), (1, 0))
            gathers[kind, e, half, 1].wait_recv()
            gather_send(kind, e, half, 3, pl.ds(half * HALF + QUARTER, QUARTER), block(half, 1, 0), (-1, 0))
            for r in (1, 3):
                gather_send(kind, e, half, 4 + r, cols, block(half, r, 0), (0, 1))
                gather_send(kind, e, half, 8 + r, cols, block(half, r, 0), (0, -1))

    def gather_3(kind, e):
        for half in range(2):
            cols = columns(half)
            gathers[kind, e, half, 2].wait_recv()
            gathers[kind, e, half, 3].wait_recv()
            gather_send(kind, e, half, 6, cols, block(half, 2, 0), (0, 1))
            gather_send(kind, e, half, 10, cols, block(half, 2, 0), (0, -1))

    def gather_4(kind, e):
        for r in (0, 1, 3, 2):
            for half in range(2):
                cols = columns(half)
                gathers[kind, e, half, 4 + r].wait_recv()
                gathers[kind, e, half, 8 + r].wait_recv()
                if r < 2:
                    gather_send(kind, e, half, 12 + r, cols, block(half, r, -1), (0, 1))
                else:
                    gather_send(kind, e, half, 12 + r, cols, block(half, r, 1), (0, -1))

    def gather_5(kind, e):
        for half in range(2):
            for r in range(4):
                gathers[kind, e, half, 12 + r].wait_recv()
            for index in range(16):
                gathers[kind, e, half, index].wait_send()

    loads = []

    def load_start():
        for e in range(OWN):
            loads.append(
                (
                    pltpu.make_async_copy(gate_hbm.at[e], gate_up.at[e, :, pl.ds(0, HID)], load_sem.at[e, 0]),
                    pltpu.make_async_copy(up_hbm.at[e], gate_up.at[e, :, pl.ds(HID, HID)], load_sem.at[e, 1]),
                    pltpu.make_async_copy(down_hbm.at[e], down.at[e], load_sem.at[e, 2]),
                )
            )
        for group in loads:
            for copy in group:
                copy.start()

    stores = {}

    def compute(e):
        for copy in loads[e]:
            copy.wait()
        if e > 0:
            for copy in stores[e - 1]:
                copy.wait()
        group = 8
        tile = group * SRC

        @pl.loop(0, N_DP // group)
        def _(j):
            blocks = pl.ds(j * group, group)
            out_rows = pl.ds(pl.multiple_of(j * tile, tile), tile)
            inputs = rows[e, blocks, 0:SRC, :].reshape(tile, D)
            both = jnp.dot(inputs, gate_up[e], preferred_element_type=F32)
            outer = rows[e, blocks, SRC:BLK, :].reshape(tile, D)
            grad_hidden = lax.dot_general(outer, down[e], NT, preferred_element_type=F32)
            gate_pre, up_value = both[:, :HID], both[:, HID:]
            sigmoid = jax.nn.sigmoid(gate_pre)
            activated = gate_pre * sigmoid
            hidden[out_rows, :] = (activated * up_value).astype(BF16)
            grads[out_rows, 0:HID] = (
                grad_hidden * up_value * sigmoid * (1.0 + gate_pre * (1.0 - sigmoid))
            ).astype(BF16)
            grads[out_rows, HID : 2 * HID] = (grad_hidden * activated).astype(BF16)

        @pl.loop(0, D // 256)
        def _(j):
            cols = pl.ds(pl.multiple_of(j * 256, 256), 256)
            inputs = rows[e, :, 0:SRC, cols].reshape(N_DP * SRC, 256)
            stage_gate_up[cols, :] = lax.dot_general(
                inputs, grads[...], TN, preferred_element_type=F32
            ).astype(BF16)
            outer = rows[e, :, SRC:BLK, cols].reshape(N_DP * SRC, 256)
            down[OWN, :, cols] = lax.dot_general(
                hidden[...], outer, TN, preferred_element_type=F32
            ).astype(BF16)

        stores[e] = (
            pltpu.make_async_copy(stage_gate_up.at[:, pl.ds(0, HID)], grad_gate_hbm.at[e], store_sem.at[e, 0]),
            pltpu.make_async_copy(stage_gate_up.at[:, pl.ds(HID, HID)], grad_up_hbm.at[e], store_sem.at[e, 1]),
            pltpu.make_async_copy(stage_down, grad_down_hbm.at[e], store_sem.at[e, 2]),
        )
        for copy in stores[e]:
            copy.start()

        for half in range(2):

            @pl.loop(half * (HALF // 256), (half + 1) * (HALF // 256))
            def _(j):
                cols = pl.ds(pl.multiple_of(j * 256, 256), 256)
                out = jnp.dot(hidden[...], down[e, :, cols], preferred_element_type=F32)
                rows[e, :, 0:SRC, cols] = out.astype(BF16).reshape(N_DP, SRC, 256)
                back = lax.dot_general(
                    grads[...], gate_up[e, cols, :], NT, preferred_element_type=F32
                )
                rows[e, :, SRC:BLK, cols] = back.astype(BF16).reshape(N_DP, SRC, 256)

            reduce_1(e, half)

    reduces = {}

    def reduce_send(e, half, index, src, dst, steps):
        target = device(half, *steps)
        copy = remote(src, dst, r_ssem.at[e, half, index], r_rsem.at[e, half, index], (target, seq))
        reduces[e, half, index] = copy

    def part(e, half, r1, r2):
        return rows.at[e, block(half, r1, r2), :, columns(half)]

    def reduce_1(e, half):
        for r in range(4):
            step = 1 if r < 2 else -1
            reduce_send(e, half, r, part(e, half, r, 2), first_far.at[e, half, r], (0, step))
        for r in (2, 3):
            reduce_send(e, half, 4 + r, part(e, half, r, 1), first_near.at[e, half, 0, r], (0, 1))
        for r in (0, 1):
            reduce_send(e, half, 8 + r, part(e, half, r, -1), first_near.at[e, half, 1, r], (0, -1))

    def reduce_2(e):
        for r in range(4):
            for half in range(2):
                step = 1 if r < 2 else -1
                reduces[e, half, r].wait_recv()
                mine = part(e, half, r, step)
                add_rows(mine, [mine, first_far.at[e, half, r]])
                way = 0 if r < 2 else 1
                reduce_send(
                    e, half, 4 + 4 * way + r, mine, first_near.at[e, half, way, r], (0, step)
                )

    def reduce_3(e):
        for r in (2, 1, 3, 0):
            for half in range(2):
                reduces[e, half, 4 + r].wait_recv()
                reduces[e, half, 8 + r].wait_recv()
                mine = part(e, half, r, 0)
                add_rows(
                    mine, [mine, first_near.at[e, half, 0, r], first_near.at[e, half, 1, r]]
                )
                if r == 2:
                    for way, step in ((0, 1), (1, -1)):
                        quarter = pl.ds(half * HALF + way * QUARTER, QUARTER)
                        src = rows.at[e, block(half, 2, 0), :, quarter]
                        reduce_send(e, half, 12 + way, src, second_far.at[e, half, way], (step, 0))

    def reduce_4(e):
        for half in range(2):
            for way, step in ((0, 1), (1, -1)):
                reduces[e, half, 12 + way].wait_recv()
                quarter = pl.ds(half * HALF + way * QUARTER, QUARTER)
                mine = rows.at[e, block(half, step, 0), :, quarter]
                add_rows(mine, [mine, second_far.at[e, half, way]])
                reduce_send(
                    e, half, 14 + way, part(e, half, step, 0), second_near.at[e, half, way], (step, 0)
                )

    returned = {}

    def reduce_5(e):
        for half in range(2):
            for way in range(2):
                reduces[e, half, 14 + way].wait_recv()
            mine = part(e, half, 0, 0)
            add_rows(mine, [mine, second_near.at[e, half, 0], second_near.at[e, half, 1]])
        back_send[e] = (
            jnp.dot(expand_ref[...], rows[e, me], preferred_element_type=F32)
            .astype(BF16)
            .reshape(N_SEQ, PACK, D)
        )
        for offset in range(1, N_SEQ):
            peer = (seq + offset) % N_SEQ
            returned[e, offset] = remote(
                back_send.at[e, peer],
                back_recv.at[seq, pl.ds(e * PACK, PACK)],
                b_ssem.at[e, offset],
                b_rsem.at[e, offset],
                (me, peer),
            )
        back_recv[seq, e * PACK : (e + 1) * PACK, :] = back_send[e, seq]

    def attention_part(queries, keys, values, bias, same):
        scores = lax.dot_general(queries, keys, NT, preferred_element_type=F32) * HD ** (-0.5)
        scores = jnp.where(same, scores + bias, -1e30)
        row_max = jnp.max(scores, axis=-1, keepdims=True)
        raised = jnp.exp(scores - row_max)
        probability = (raised / jnp.sum(raised, axis=-1, keepdims=True)).astype(BF16)
        return jnp.dot(probability, values, preferred_element_type=F32).astype(BF16)

    places = send_places(ids_ref)
    cot = cot_ref[...].astype(F32)
    packed = None
    for k in range(TOPK):
        grad_out = (as_column(weight_ref[k : k + 1, :]) * cot).astype(BF16)
        term = jnp.dot(places[k].astype(BF16), grad_out, preferred_element_type=F32)
        packed = term if packed is None else packed + term
    exchange_build(1, packed.astype(BF16))
    meta[seq] = jnp.concatenate(
        [bias_ref[...], mem_session_ref[...].astype(F32), jnp.zeros((8 - KVH - 1, MEM), F32)],
        axis=0,
    )
    for copy in own_loads:
        copy.wait()
    pl.semaphore_wait(barrier, 6 + N_SEQ - 1)

    meta_copies = []
    for offset in range(1, N_SEQ):
        peer = (seq + offset) % N_SEQ
        meta_copies.append(
            remote(meta.at[seq], meta.at[seq], m_ssem.at[offset], m_rsem.at[offset], (me, peer))
        )
    output_1()
    ring_1(0)
    exchange_start(1)
    output_2()
    ring_2(0)
    output_3()
    ring_1(1)
    exchange_end(1)
    for e in range(OWN):
        gather_1(1, e)
    ring_3(0)
    ring_4(0)
    stage_gate_up[own_rows, :] = jnp.dot(
        memory[...], gate_up[0], preferred_element_type=F32
    ).astype(BF16)
    ring_1(3)
    ring_2(1)
    for e in range(OWN):
        gather_2(1, e)
    ring_2(3)
    ring_3(1)
    for e in range(OWN):
        gather_3(1, e)
    output_4()
    ring_3(3)
    ring_4(1)
    tokens = tokens_ref[...]
    queries = [
        jnp.dot(tokens, gate_up[1 + g], preferred_element_type=F32).astype(BF16) for g in range(KVH)
    ]
    for copy in meta_copies:
        copy.wait()
    ring_4(3)
    session_all = jnp.concatenate([meta[s, 2:3, :] for s in range(N_SEQ)], axis=1)
    own_session = as_column(session_ref[...].astype(F32))
    same = jnp.concatenate([own_session, own_session], axis=0) == session_all
    mixed = []
    for g in range(KVH):
        keys = stage_gate_up[:, g * HD : (g + 1) * HD]
        values = stage_gate_up[:, (KVH + g) * HD : (KVH + g + 1) * HD]
        bias = jnp.concatenate([meta[s, g : g + 1, :] for s in range(N_SEQ)], axis=1)
        for pair in range(2):
            first = queries[g][:, pair * 2 * HD : (pair * 2 + 1) * HD]
            second = queries[g][:, (pair * 2 + 1) * HD : (pair * 2 + 2) * HD]
            both = attention_part(
                jnp.concatenate([first, second], axis=0), keys, values, bias, same
            )
            mixed.extend([both[0:TOK], both[TOK : 2 * TOK]])
    output_5()
    mixed = jnp.concatenate(mixed, axis=1)
    projected = jnp.dot(
        mixed, down[...].reshape((OWN + 1) * HID, D), preferred_element_type=F32
    )
    residual_keep[...] = (tokens.astype(F32) + projected).astype(BF16)
    residual = residual_keep[...].astype(F32)
    inv_rms = lax.rsqrt(jnp.mean(residual * residual, axis=-1, keepdims=True) + 1e-05)
    moe_in = (residual * inv_rms * gain_ref[...]).astype(BF16)
    either = (places[0] + places[1]).astype(BF16)
    exchange_build(0, jnp.dot(either, moe_in, preferred_element_type=F32).astype(BF16))
    exchange_start(0)
    for which in (0, 1, 2, 3):
        ring_sent(which)
    output_sent()
    load_start()
    for e in range(OWN):
        gather_4(1, e)
    exchange_end(0)
    gather_1(0, 0)
    gather_1(0, 1)
    gather_1(0, 2)
    gather_2(0, 0)
    gather_2(0, 1)
    gather_2(0, 2)
    gather_3(0, 0)
    gather_3(0, 1)
    gather_3(0, 2)
    for e in range(OWN):
        gather_5(1, e)
    gather_4(0, 0)
    gather_4(0, 1)
    gather_4(0, 2)
    gather_5(0, 0)
    compute(0)
    gather_5(0, 1)
    compute(1)
    reduce_2(0)
    gather_5(0, 2)
    compute(2)
    reduce_2(1)
    reduce_3(0)
    reduce_2(2)
    reduce_3(1)
    reduce_4(0)
    reduce_3(2)
    reduce_5(0)
    reduce_4(1)
    reduce_4(2)
    reduce_5(1)
    reduce_5(2)
    for copy in returned.values():
        copy.wait()
    for copy in reduces.values():
        copy.wait_send()
    for copy in stores[OWN - 1]:
        copy.wait()


def finish(ids, weights, back, residual, cot, gain, grads):
    vmem = pl.BlockSpec(memory_space=pltpu.VMEM)
    hbm = pl.BlockSpec(memory_space=pl.ANY)
    return pl.pallas_call(
        finish_kernel,
        out_shape=(
            jax.ShapeDtypeStruct((TOK, D), BF16),
            jax.ShapeDtypeStruct((TOK, D), BF16),
        )
        + tuple(jax.ShapeDtypeStruct(g.shape, BF16) for g in grads),
        in_specs=[vmem] * 6 + [hbm] * 3,
        out_specs=(vmem, vmem, hbm, hbm, hbm),
        scratch_shapes=[pltpu.VMEM(g.shape, BF16) for g in grads]
        + [pltpu.SemaphoreType.DMA((OWN, 3)), pltpu.SemaphoreType.DMA((OWN, 3))],
        compiler_params=pltpu.CompilerParams(vmem_limit_bytes=63 * 2**20),
        name="finish",
    )(ids, weights, back, residual, cot, gain, *grads)


def decoder_block(
    tokens, memory, bias, mem_session, session, cot, gain, ids, weights, projections, experts
):
    vmem = pl.BlockSpec(memory_space=pltpu.VMEM)
    hbm = pl.BlockSpec(memory_space=pl.ANY)
    corner = corner_matrix()
    dma = pltpu.SemaphoreType.DMA
    return pl.pallas_call(
        block_kernel,
        out_shape=(
            jax.ShapeDtypeStruct((N_SEQ, OWN * PACK, D), BF16),
            jax.ShapeDtypeStruct((TOK, D), BF16),
        )
        + tuple(jax.ShapeDtypeStruct(w.shape, BF16) for w in experts),
        in_specs=[vmem] * 12 + [hbm] * 7,
        out_specs=(vmem, vmem, hbm, hbm, hbm),
        scratch_shapes=[
            pltpu.VMEM((OWN, N_DP, BLK, D), BF16),
            pltpu.VMEM((OWN, D, 2 * HID), BF16),
            pltpu.VMEM((OWN + 1, HID, D), BF16),
            pltpu.VMEM((N_DP * SRC, HID), BF16),
            pltpu.VMEM((N_DP * SRC, 2 * HID), BF16),
            pltpu.VMEM((D, 2 * HID), BF16),
            pltpu.VMEM((MEM, D), BF16),
            pltpu.VMEM((N_SEQ, 8, MEM), F32),
            pltpu.VMEM((2, N_SEQ, 16, WIDE), BF16),
            pltpu.VMEM((2, N_SEQ, 16, WIDE), BF16),
            pltpu.VMEM((OWN, N_SEQ, PACK, D), BF16),
            pltpu.VMEM((OWN, 2, 4, BLK, HALF), BF16),
            pltpu.VMEM((OWN, 2, 2, 4, BLK, HALF), BF16),
            pltpu.VMEM((OWN, 2, 2, BLK, QUARTER), BF16),
            pltpu.VMEM((OWN, 2, 2, BLK, HALF), BF16),
            dma((5,)),
            dma((OWN, 3)),
            dma((OWN, 3)),
            dma((N_SEQ,)),
            dma((N_SEQ,)),
            dma((2, 3, 3)),
            dma((2, 3, 3)),
            dma((5, 8)),
            dma((5, 8)),
            dma((2, N_SEQ)),
            dma((2, N_SEQ)),
            dma((OWN, N_SEQ)),
            dma((OWN, N_SEQ)),
            dma((2, OWN, 2, 16)),
            dma((2, OWN, 2, 16)),
            dma((OWN, 2, 16)),
            dma((OWN, 2, 16)),
        ],
        compiler_params=pltpu.CompilerParams(
            collective_id=1, has_side_effects=True, vmem_limit_bytes=63 * 2**20
        ),
        name="decoder_block",
    )(
        tokens,
        bias,
        mem_session,
        session,
        cot,
        gain,
        ids,
        weights,
        jnp.asarray(compact_matrix(), BF16),
        jnp.asarray(corner, BF16),
        jnp.asarray(corner.T, BF16),
        jnp.asarray(return_matrix().T, BF16),
        memory,
        *projections,
        *experts,
    )


def per_device(
    tokens,
    memory,
    mem_session,
    dec_session,
    event_bias,
    expert_ids,
    route_weights,
    norm_gain,
    w_query,
    w_keyval,
    w_output,
    w_gate,
    w_up,
    w_down,
    cotangent,
):
    ids, weights = expert_ids[0].T, route_weights[0].T
    gain = norm_gain.reshape(1, D)
    back, residual, *grads = decoder_block(
        tokens[0],
        memory[0],
        event_bias[0],
        mem_session,
        dec_session,
        cotangent[0],
        gain,
        ids,
        weights,
        (w_query, w_keyval, w_output),
        (w_gate, w_up, w_down),
    )
    block_out, grad_resid, grad_gate, grad_up, grad_down = finish(
        ids, weights, back, residual, cotangent[0], gain, grads
    )
    return (block_out[None], grad_resid[None], grad_gate, grad_up, grad_down)


def solution(mesh):
    return jax.shard_map(
        per_device,
        mesh=mesh,
        in_specs=(
            P("dp", "seq", None),
            P("dp", "seq", None),
            P("dp", "seq"),
            P("dp", "seq"),
            P("dp", None, "seq"),
            P("dp", "seq", None),
            P("dp", "seq", None),
            P(),
            P("seq", None),
            P("seq", None),
            P("seq", None),
            P("seq", None, "dp"),
            P("seq", None, "dp"),
            P("seq", "dp", None),
            P("dp", "seq", None),
        ),
        out_specs=(
            P("dp", "seq", None),
            P("dp", "seq", None),
            P("seq", None, "dp"),
            P("seq", None, "dp"),
            P("seq", "dp", None),
        ),
        check_vma=False,
    )
```

```python
import functools

import jax
import jax.numpy as jnp
import numpy as np
from jax import lax
from jax.experimental import pallas as pl
from jax.experimental.pallas import tpu as pltpu
from jax.sharding import PartitionSpec as P

D = 2048
EXPERTS = 24
TOPK = 2
QH = 8
KVH = 2
HD = 128
CAP = 6
SIDE = 4
N_DP = 16
N_SEQ = 8
OWN = 3
HID = 256
TOK = 64
SRC = N_SEQ * CAP
BLK = 2 * SRC
PACK = 16
MEM = 256
WIDE = D + 256
KV = 2 * KVH * HD
STRIP = HD // 4
HALF = D // 2
QUARTER = D // 4
MESH = pl.DeviceIdType.MESH
F32 = jnp.float32
BF16 = jnp.bfloat16
NT = (((1,), (1,)), ((), ()))
TN = (((0,), (0,)), ((), ()))


def return_matrix():
    table = np.zeros((BLK, N_SEQ * PACK), np.float32)
    for kind in range(2):
        for source in range(N_SEQ):
            for slot in range(CAP):
                table[kind * SRC + source * CAP + slot, source * PACK + kind * CAP + slot] = 1.0
    return table


def compact_matrix():
    table = np.zeros((OWN * SRC, OWN * SRC), np.float32)
    for expert in range(OWN):
        for source in range(N_SEQ):
            for slot in range(CAP):
                row = expert * CAP + slot
                column = source * 16 + row if row < 16 else N_SEQ * 16 + source * 2 + row - 16
                table[expert * SRC + source * CAP + slot, column] = 1.0
    return table


def corner_matrix():
    table = np.zeros((N_SEQ * 16, N_SEQ * 16), np.float32)
    for piece in range(8):
        for peer in range(N_SEQ):
            for last in range(2):
                table[peer * 16 + piece * 2 + last, piece * 16 + peer * 2 + last] = 1.0
    return table


def squares():
    down = lax.broadcasted_iota(jnp.int32, (TOK, TOK), 0)
    across = lax.broadcasted_iota(jnp.int32, (TOK, TOK), 1)
    return down, across


def as_column(row):
    down, across = squares()
    return jnp.sum(jnp.where(down == across, row, 0.0), axis=1, keepdims=True)


def one_hot(mask):
    return jnp.where(mask, 1.0, 0.0).astype(BF16)


def routed(ids_ref):
    down, across = squares()
    row = [ids_ref[k : k + 1, :].astype(F32) for k in range(TOPK)]
    column = [as_column(r) for r in row]

    def earlier(own, others, before, axis):
        named = sum(jnp.where(own == other, 1.0, 0.0) for other in others)
        return jnp.sum(jnp.where(before, named, 0.0), axis=axis, keepdims=True)

    row_slot = [earlier(row[k], column, down < across, 0) for k in range(TOPK)]
    column_slot = [earlier(column[k], row, across < down, 1) for k in range(TOPK)]
    return row, row_slot, column, column_slot


def send_places(ids_ref):
    row, row_slot, _, _ = routed(ids_ref)
    every = lax.broadcasted_iota(jnp.int32, (N_SEQ * 18, TOK), 0).astype(F32)
    places = []
    for k in range(TOPK):
        owner = jnp.floor((row[k] + 0.5) * (1.0 / OWN))
        place = (row[k] - OWN * owner) * CAP + row_slot[k]
        target = jnp.where(
            place < 16, owner * 16 + place, N_SEQ * 16 + owner * 2 + place - 16
        )
        places.append(jnp.where(every == target, 1.0, 0.0))
    return places


def add_rows(out, terms):
    @pl.loop(0, BLK // 16)
    def _(i):
        rows = pl.ds(pl.multiple_of(i * 16, 16), 16)
        total = terms[0][rows, :].astype(F32)
        for term in terms[1:]:
            total = total + term[rows, :].astype(F32)
        out[rows, :] = total.astype(BF16)


def finish_kernel(
    ids_ref,
    weight_ref,
    back_ref,
    residual_ref,
    cot_ref,
    gain_ref,
    gate_in,
    up_in,
    down_in,
    block_out_ref,
    grad_resid_ref,
    gate_out,
    up_out,
    down_out,
    gate_via,
    up_via,
    down_via,
    in_sem,
    out_sem,
):
    loads, copies = [], []
    for e in range(OWN):
        for i, (src, via, dst) in enumerate(
            ((gate_in, gate_via, gate_out), (up_in, up_via, up_out), (down_in, down_via, down_out))
        ):
            loads.append(pltpu.make_async_copy(src.at[e], via.at[e], in_sem.at[e, i]))
            copies.append(pltpu.make_async_copy(via.at[e], dst.at[e], out_sem.at[e, i]))
    for load in loads:
        load.start()
    _, _, column, column_slot = routed(ids_ref)
    every = lax.broadcasted_iota(jnp.int32, (TOK, EXPERTS * PACK), 1).astype(F32)
    back = back_ref[...].reshape(EXPERTS * PACK, D)
    answers = [column[k] * PACK + column_slot[k] for k in range(TOPK)]
    residual = residual_ref[...].astype(F32)
    combined = None
    for k in range(TOPK):
        picked = jnp.dot(one_hot(every == answers[k]), back, preferred_element_type=F32)
        term = picked * as_column(weight_ref[k : k + 1, :])
        combined = term if combined is None else combined + term
    block_out_ref[...] = (residual + combined).astype(BF16)
    both = (every == answers[0] + CAP) | (every == answers[1] + CAP)
    grad_moe = jnp.dot(one_hot(both), back, preferred_element_type=F32)
    inv_rms = lax.rsqrt(jnp.mean(residual * residual, axis=-1, keepdims=True) + 1e-05)
    normed = residual * inv_rms
    grad_normed = grad_moe * gain_ref[...]
    correction = normed * jnp.mean(grad_normed * normed, axis=-1, keepdims=True)
    grad_resid_ref[...] = (
        cot_ref[...].astype(F32) + inv_rms * (grad_normed - correction)
    ).astype(BF16)
    for load, copy in zip(loads, copies):
        load.wait()
        copy.start()
    for copy in copies:
        copy.wait()


def block_kernel(
    tokens_ref,
    bias_ref,
    mem_session_ref,
    session_ref,
    cot_ref,
    gain_ref,
    ids_ref,
    weight_ref,
    compact_ref,
    corner_ref,
    corner_back_ref,
    expand_ref,
    memory_hbm,
    query_hbm,
    keyval_hbm,
    output_hbm,
    gate_hbm,
    up_hbm,
    down_hbm,
    back_recv,
    residual_keep,
    grad_gate_hbm,
    grad_up_hbm,
    grad_down_hbm,
    rows,
    gate_up,
    down,
    hidden,
    grads,
    stage_gate_up,
    memory,
    meta,
    z_send,
    z_recv,
    back_send,
    first_far,
    first_near,
    second_far,
    second_near,
    own_sem,
    load_sem,
    store_sem,
    m_ssem,
    m_rsem,
    s_ssem,
    s_rsem,
    w_ssem,
    w_rsem,
    z_ssem,
    z_rsem,
    b_ssem,
    b_rsem,
    g_ssem,
    g_rsem,
    r_ssem,
    r_rsem,
):
    me = lax.axis_index("dp")
    seq = lax.axis_index("seq")
    mx, my = me // SIDE, me % SIDE
    mz, mc = seq // 2, seq % 2
    stage_down = down.at[OWN]

    def device(half, step1, step2):
        dx, dy = (step1, step2) if half == 0 else (step2, step1)
        return ((mx + dx + SIDE) % SIDE) * SIDE + (my + dy + SIDE) % SIDE

    def columns(half):
        return pl.ds(half * HALF, HALF)

    barrier = pltpu.get_barrier_semaphore()
    for half in range(2):
        for step in (1, -1, 2):
            pl.semaphore_signal(
                barrier, inc=1, device_id=(device(half, step, 0), seq), device_id_type=MESH
            )
    for offset in range(1, N_SEQ):
        pl.semaphore_signal(
            barrier, inc=1, device_id=(me, (seq + offset) % N_SEQ), device_id_type=MESH
        )

    def remote(src, dst, ssem, rsem, target):
        copy = pltpu.make_async_remote_copy(
            src_ref=src,
            dst_ref=dst,
            send_sem=ssem,
            recv_sem=rsem,
            device_id=target,
            device_id_type=MESH,
        )
        copy.start()
        return copy

    own_rows = pl.ds(seq * MEM, MEM)
    own_loads = [
        pltpu.make_async_copy(keyval_hbm, gate_up.at[0, own_rows, :], own_sem.at[0]),
        pltpu.make_async_copy(query_hbm.at[:, pl.ds(0, KV)], gate_up.at[1, own_rows, :], own_sem.at[1]),
        pltpu.make_async_copy(query_hbm.at[:, pl.ds(KV, KV)], gate_up.at[2, own_rows, :], own_sem.at[2]),
        pltpu.make_async_copy(output_hbm, down.at[mz, pl.ds(mc * HD, HD), :], own_sem.at[3]),
        pltpu.make_async_copy(memory_hbm, memory, own_sem.at[4]),
    ]
    for copy in own_loads:
        copy.start()

    z_copies = {}

    def exchange_build(kind, packed):
        z_send[kind, :, :, 0:D] = packed[0 : N_SEQ * 16].reshape(N_SEQ, 16, D)
        last = packed[N_SEQ * 16 :]
        pieces = jnp.concatenate([last[:, i * 256 : (i + 1) * 256] for i in range(8)], axis=0)
        corner = jnp.dot(corner_ref[...], pieces, preferred_element_type=F32).astype(BF16)
        z_send[kind, :, :, D:WIDE] = corner.reshape(N_SEQ, 16, 256)

    def exchange_start(kind):
        for offset in range(1, N_SEQ):
            peer = (seq + offset) % N_SEQ
            z_copies[kind, offset] = remote(
                z_send.at[kind, peer],
                z_recv.at[kind, seq],
                z_ssem.at[kind, offset],
                z_rsem.at[kind, offset],
                (me, peer),
            )
        z_recv[kind, seq] = z_send[kind, seq]

    def exchange_end(kind):
        for offset in range(1, N_SEQ):
            z_copies[kind, offset].wait()
        first = z_recv[kind, :, :, 0:D].reshape(N_SEQ * 16, D)
        corner = z_recv[kind, :, :, D:WIDE].reshape(N_SEQ * 16, 256)
        pieces = jnp.dot(corner_back_ref[...], corner, preferred_element_type=F32).astype(BF16)
        last = jnp.concatenate([pieces[i * 16 : (i + 1) * 16] for i in range(8)], axis=1)
        arrived = jnp.concatenate([first, last], axis=0)
        compact = jnp.dot(compact_ref[...], arrived, preferred_element_type=F32).astype(BF16)
        for e in range(OWN):
            rows[e, me, kind * SRC : (kind + 1) * SRC, :] = compact[e * SRC : (e + 1) * SRC]

    ring = {}

    def keyval_weight_region(zz, cc, start, size):
        return gate_up.at[0, pl.ds((zz * 2 + cc) * MEM + start, size), :]

    def query_weight_region(zz, cc, start, size):
        return gate_up.at[pl.ds(1, 2), pl.ds((zz * 2 + cc) * MEM + start, size), :]

    def keyval_region(zz, cc, start, size):
        return stage_gate_up.at[pl.ds((zz * 2 + cc) * MEM + start, size), :]

    regions = [
        (keyval_weight_region, MEM),
        (query_weight_region, MEM),
        None,
        (keyval_region, MEM),
    ]

    def ring_send(which, index, dz_owner, start, size, step, core):
        ref = regions[which][0]((mz + dz_owner + SIDE) % SIDE, mc, start, size)
        target = (me, ((mz + step + SIDE) % SIDE) * 2 + core)
        ring[which, index] = remote(ref, ref, w_ssem.at[which, index], w_rsem.at[which, index], target)

    def ring_1(which):
        size = regions[which][1]
        ring_send(which, 0, 0, 0, size, 1, mc)
        ring_send(which, 1, 0, 0, size, -1, mc)
        ring_send(which, 4, 0, 0, size, 0, 1 - mc)

    def ring_2(which):
        size = regions[which][1]
        ring[which, 0].wait_recv()
        ring_send(which, 2, -1, 0, size // 2, 1, mc)
        ring_send(which, 5, -1, 0, size, 0, 1 - mc)
        ring[which, 1].wait_recv()
        ring_send(which, 3, 1, size // 2, size // 2, -1, mc)
        ring_send(which, 6, 1, 0, size, 0, 1 - mc)

    def ring_3(which):
        ring[which, 2].wait_recv()
        ring[which, 3].wait_recv()
        ring_send(which, 7, 2, 0, regions[which][1], 0, 1 - mc)

    def ring_4(which):
        for index in range(4, 8):
            ring[which, index].wait_recv()

    def ring_sent(which):
        for index in range(8):
            ring[which, index].wait_send()

    spread = {}
    others = (-1, 1, 2)

    def quarter_of(dz_owner, half, start, size):
        place = mc * HD + (mx if half == 0 else my) * STRIP + start
        return down.at[(mz + dz_owner + SIDE) % SIDE, pl.ds(place, size), columns(half)]

    def strip_send(half, index, dz_owner, start, size, step):
        ref = quarter_of(dz_owner, half, start, size)
        which = 2 + 2 * half
        target = (me, ((mz + step + SIDE) % SIDE) * 2 + mc)
        ring[which, index] = remote(ref, ref, w_ssem.at[which, index], w_rsem.at[which, index], target)

    def shard_to_sibling(index, dz_owner):
        ref = down.at[(mz + dz_owner + SIDE) % SIDE, pl.ds(mc * HD, HD), :]
        ring[2, index] = remote(
            ref, ref, w_ssem.at[2, index], w_rsem.at[2, index], (me, mz * 2 + 1 - mc)
        )

    def strip_spread(half, other):
        ref = quarter_of(others[other], half, 0, STRIP)
        for peer in range(3):
            spread[half, other, peer] = remote(
                ref,
                ref,
                s_ssem.at[half, other, peer],
                s_rsem.at[half, other, peer],
                (device(half, others[peer], 0), seq),
            )

    def output_1():
        for half in range(2):
            strip_send(half, 0, 0, 0, STRIP, 1)
            strip_send(half, 1, 0, 0, STRIP, -1)
        shard_to_sibling(4, 0)

    def output_2():
        for half in range(2):
            ring[2 + 2 * half, 0].wait_recv()
            strip_send(half, 2, -1, 0, STRIP // 2, 1)
            strip_spread(half, 0)
            ring[2 + 2 * half, 1].wait_recv()
            strip_send(half, 3, 1, STRIP // 2, STRIP // 2, -1)
            strip_spread(half, 1)

    def output_3():
        for half in range(2):
            ring[2 + 2 * half, 2].wait_recv()
            ring[2 + 2 * half, 3].wait_recv()
            strip_spread(half, 2)

    def output_4():
        for other in range(3):
            for half in range(2):
                for peer in range(3):
                    spread[half, other, peer].wait_recv()
            shard_to_sibling(5 + other, others[other])

    def output_5():
        for index in range(4, 8):
            ring[2, index].wait_recv()

    def output_sent():
        for copy in spread.values():
            copy.wait_send()
        for index in range(4):
            ring[4, index].wait_send()

    def block(half, r1, r2):
        return device(half, r1, r2)

    gathers = {}

    def gather_send(kind, e, half, index, width, origin, steps):
        target = device(half, *steps)
        part = rows.at[e, origin, pl.ds(kind * SRC, SRC), width]
        copy = remote(part, part, g_ssem.at[kind, e, half, index], g_rsem.at[kind, e, half, index], (target, seq))
        gathers[kind, e, half, index] = copy

    def gather_1(kind, e):
        for half in range(2):
            cols = columns(half)
            gather_send(kind, e, half, 0, cols, me, (1, 0))
            gather_send(kind, e, half, 1, cols, me, (-1, 0))
        for half in range(2):
            cols = columns(half)
            gather_send(kind, e, half, 4, cols, me, (0, 1))
            gather_send(kind, e, half, 8, cols, me, (0, -1))

    def gather_2(kind, e):
        for half in range(2):
            cols = columns(half)
            gathers[kind, e, half, 0].wait_recv()
            gather_send(kind, e, half, 2, pl.ds(half * HALF, QUARTER), block(half, -1, 0), (1, 0))
            gathers[kind, e, half, 1].wait_recv()
            gather_send(kind, e, half, 3, pl.ds(half * HALF + QUARTER, QUARTER), block(half, 1, 0), (-1, 0))
            for r in (1, 3):
                gather_send(kind, e, half, 4 + r, cols, block(half, r, 0), (0, 1))
                gather_send(kind, e, half, 8 + r, cols, block(half, r, 0), (0, -1))

    def gather_3(kind, e):
        for half in range(2):
            cols = columns(half)
            gathers[kind, e, half, 2].wait_recv()
            gathers[kind, e, half, 3].wait_recv()
            gather_send(kind, e, half, 6, cols, block(half, 2, 0), (0, 1))
            gather_send(kind, e, half, 10, cols, block(half, 2, 0), (0, -1))

    def gather_4(kind, e):
        for r in (0, 1, 3, 2):
            for half in range(2):
                cols = columns(half)
                gathers[kind, e, half, 4 + r].wait_recv()
                gathers[kind, e, half, 8 + r].wait_recv()
                if r < 2:
                    gather_send(kind, e, half, 12 + r, cols, block(half, r, -1), (0, 1))
                else:
                    gather_send(kind, e, half, 12 + r, cols, block(half, r, 1), (0, -1))

    def gather_5(kind, e):
        for half in range(2):
            for r in range(4):
                gathers[kind, e, half, 12 + r].wait_recv()
            for index in range(16):
                gathers[kind, e, half, index].wait_send()

    loads = []

    def load_start():
        for e in range(OWN):
            loads.append(
                (
                    pltpu.make_async_copy(gate_hbm.at[e], gate_up.at[e, :, pl.ds(0, HID)], load_sem.at[e, 0]),
                    pltpu.make_async_copy(up_hbm.at[e], gate_up.at[e, :, pl.ds(HID, HID)], load_sem.at[e, 1]),
                    pltpu.make_async_copy(down_hbm.at[e], down.at[e], load_sem.at[e, 2]),
                )
            )
        for group in loads:
            for copy in group:
                copy.start()

    stores = {}

    def compute(e):
        for copy in loads[e]:
            copy.wait()
        if e > 0:
            for copy in stores[e - 1]:
                copy.wait()
        group = 8
        tile = group * SRC

        @pl.loop(0, N_DP // group)
        def _(j):
            blocks = pl.ds(j * group, group)
            out_rows = pl.ds(pl.multiple_of(j * tile, tile), tile)
            inputs = rows[e, blocks, 0:SRC, :].reshape(tile, D)
            both = jnp.dot(inputs, gate_up[e], preferred_element_type=F32)
            outer = rows[e, blocks, SRC:BLK, :].reshape(tile, D)
            grad_hidden = lax.dot_general(outer, down[e], NT, preferred_element_type=F32)
            gate_pre, up_value = both[:, :HID], both[:, HID:]
            sigmoid = jax.nn.sigmoid(gate_pre)
            activated = gate_pre * sigmoid
            hidden[out_rows, :] = (activated * up_value).astype(BF16)
            grads[out_rows, 0:HID] = (
                grad_hidden * up_value * sigmoid * (1.0 + gate_pre * (1.0 - sigmoid))
            ).astype(BF16)
            grads[out_rows, HID : 2 * HID] = (grad_hidden * activated).astype(BF16)

        @pl.loop(0, D // 256)
        def _(j):
            cols = pl.ds(pl.multiple_of(j * 256, 256), 256)
            inputs = rows[e, :, 0:SRC, cols].reshape(N_DP * SRC, 256)
            stage_gate_up[cols, :] = lax.dot_general(
                inputs, grads[...], TN, preferred_element_type=F32
            ).astype(BF16)
            outer = rows[e, :, SRC:BLK, cols].reshape(N_DP * SRC, 256)
            down[OWN, :, cols] = lax.dot_general(
                hidden[...], outer, TN, preferred_element_type=F32
            ).astype(BF16)

        stores[e] = (
            pltpu.make_async_copy(stage_gate_up.at[:, pl.ds(0, HID)], grad_gate_hbm.at[e], store_sem.at[e, 0]),
            pltpu.make_async_copy(stage_gate_up.at[:, pl.ds(HID, HID)], grad_up_hbm.at[e], store_sem.at[e, 1]),
            pltpu.make_async_copy(stage_down, grad_down_hbm.at[e], store_sem.at[e, 2]),
        )
        for copy in stores[e]:
            copy.start()

        for half in range(2):

            @pl.loop(half * (HALF // 256), (half + 1) * (HALF // 256))
            def _(j):
                cols = pl.ds(pl.multiple_of(j * 256, 256), 256)
                out = jnp.dot(hidden[...], down[e, :, cols], preferred_element_type=F32)
                rows[e, :, 0:SRC, cols] = out.astype(BF16).reshape(N_DP, SRC, 256)
                back = lax.dot_general(
                    grads[...], gate_up[e, cols, :], NT, preferred_element_type=F32
                )
                rows[e, :, SRC:BLK, cols] = back.astype(BF16).reshape(N_DP, SRC, 256)

            reduce_1(e, half)

    reduces = {}

    def reduce_send(e, half, index, src, dst, steps):
        target = device(half, *steps)
        copy = remote(src, dst, r_ssem.at[e, half, index], r_rsem.at[e, half, index], (target, seq))
        reduces[e, half, index] = copy

    def part(e, half, r1, r2):
        return rows.at[e, block(half, r1, r2), :, columns(half)]

    def reduce_1(e, half):
        for r in range(4):
            step = 1 if r < 2 else -1
            reduce_send(e, half, r, part(e, half, r, 2), first_far.at[e, half, r], (0, step))
        for r in (2, 3):
            reduce_send(e, half, 4 + r, part(e, half, r, 1), first_near.at[e, half, 0, r], (0, 1))
        for r in (0, 1):
            reduce_send(e, half, 8 + r, part(e, half, r, -1), first_near.at[e, half, 1, r], (0, -1))

    def reduce_2(e):
        for r in range(4):
            for half in range(2):
                step = 1 if r < 2 else -1
                reduces[e, half, r].wait_recv()
                mine = part(e, half, r, step)
                add_rows(mine, [mine, first_far.at[e, half, r]])
                way = 0 if r < 2 else 1
                reduce_send(
                    e, half, 4 + 4 * way + r, mine, first_near.at[e, half, way, r], (0, step)
                )

    def reduce_3(e):
        for r in (2, 1, 3, 0):
            for half in range(2):
                reduces[e, half, 4 + r].wait_recv()
                reduces[e, half, 8 + r].wait_recv()
                mine = part(e, half, r, 0)
                add_rows(
                    mine, [mine, first_near.at[e, half, 0, r], first_near.at[e, half, 1, r]]
                )
                if r == 2:
                    for way, step in ((0, 1), (1, -1)):
                        quarter = pl.ds(half * HALF + way * QUARTER, QUARTER)
                        src = rows.at[e, block(half, 2, 0), :, quarter]
                        reduce_send(e, half, 12 + way, src, second_far.at[e, half, way], (step, 0))

    def reduce_4(e):
        for half in range(2):
            for way, step in ((0, 1), (1, -1)):
                reduces[e, half, 12 + way].wait_recv()
                quarter = pl.ds(half * HALF + way * QUARTER, QUARTER)
                mine = rows.at[e, block(half, step, 0), :, quarter]
                add_rows(mine, [mine, second_far.at[e, half, way]])
                reduce_send(
                    e, half, 14 + way, part(e, half, step, 0), second_near.at[e, half, way], (step, 0)
                )

    returned = {}

    def reduce_5(e):
        for half in range(2):
            for way in range(2):
                reduces[e, half, 14 + way].wait_recv()
            mine = part(e, half, 0, 0)
            add_rows(mine, [mine, second_near.at[e, half, 0], second_near.at[e, half, 1]])
        back_send[e] = (
            jnp.dot(expand_ref[...], rows[e, me], preferred_element_type=F32)
            .astype(BF16)
            .reshape(N_SEQ, PACK, D)
        )
        for offset in range(1, N_SEQ):
            peer = (seq + offset) % N_SEQ
            returned[e, offset] = remote(
                back_send.at[e, peer],
                back_recv.at[seq, pl.ds(e * PACK, PACK)],
                b_ssem.at[e, offset],
                b_rsem.at[e, offset],
                (me, peer),
            )
        back_recv[seq, e * PACK : (e + 1) * PACK, :] = back_send[e, seq]

    def attention_part(queries, keys, values, bias, same):
        scores = lax.dot_general(queries, keys, NT, preferred_element_type=F32) * HD ** (-0.5)
        scores = jnp.where(same, scores + bias, -1e30)
        row_max = jnp.max(scores, axis=-1, keepdims=True)
        raised = jnp.exp(scores - row_max)
        probability = (raised / jnp.sum(raised, axis=-1, keepdims=True)).astype(BF16)
        return jnp.dot(probability, values, preferred_element_type=F32).astype(BF16)

    places = send_places(ids_ref)
    cot = cot_ref[...].astype(F32)
    packed = None
    for k in range(TOPK):
        grad_out = (as_column(weight_ref[k : k + 1, :]) * cot).astype(BF16)
        term = jnp.dot(places[k].astype(BF16), grad_out, preferred_element_type=F32)
        packed = term if packed is None else packed + term
    exchange_build(1, packed.astype(BF16))
    meta[seq] = jnp.concatenate(
        [bias_ref[...], mem_session_ref[...].astype(F32), jnp.zeros((8 - KVH - 1, MEM), F32)],
        axis=0,
    )
    for copy in own_loads:
        copy.wait()
    pl.semaphore_wait(barrier, 6 + N_SEQ - 1)

    meta_copies = []
    for offset in range(1, N_SEQ):
        peer = (seq + offset) % N_SEQ
        meta_copies.append(
            remote(meta.at[seq], meta.at[seq], m_ssem.at[offset], m_rsem.at[offset], (me, peer))
        )
    output_1()
    ring_1(0)
    output_2()
    ring_2(0)
    output_3()
    exchange_start(1)
    ring_1(1)
    exchange_end(1)
    for e in range(OWN):
        gather_1(1, e)
    ring_3(0)
    ring_4(0)
    stage_gate_up[own_rows, :] = jnp.dot(
        memory[...], gate_up[0], preferred_element_type=F32
    ).astype(BF16)
    ring_1(3)
    ring_2(1)
    for e in range(OWN):
        gather_2(1, e)
    ring_2(3)
    ring_3(1)
    for e in range(OWN):
        gather_3(1, e)
    output_4()
    ring_3(3)
    ring_4(1)
    tokens = tokens_ref[...]
    queries = [
        jnp.dot(tokens, gate_up[1 + g], preferred_element_type=F32).astype(BF16) for g in range(KVH)
    ]
    for copy in meta_copies:
        copy.wait()
    ring_4(3)
    session_all = jnp.concatenate([meta[s, 2:3, :] for s in range(N_SEQ)], axis=1)
    own_session = as_column(session_ref[...].astype(F32))
    same = jnp.concatenate([own_session, own_session], axis=0) == session_all
    mixed = []
    for g in range(KVH):
        keys = stage_gate_up[:, g * HD : (g + 1) * HD]
        values = stage_gate_up[:, (KVH + g) * HD : (KVH + g + 1) * HD]
        bias = jnp.concatenate([meta[s, g : g + 1, :] for s in range(N_SEQ)], axis=1)
        for pair in range(2):
            first = queries[g][:, pair * 2 * HD : (pair * 2 + 1) * HD]
            second = queries[g][:, (pair * 2 + 1) * HD : (pair * 2 + 2) * HD]
            both = attention_part(
                jnp.concatenate([first, second], axis=0), keys, values, bias, same
            )
            mixed.extend([both[0:TOK], both[TOK : 2 * TOK]])
    output_5()
    mixed = jnp.concatenate(mixed, axis=1)
    projected = jnp.dot(
        mixed, down[...].reshape((OWN + 1) * HID, D), preferred_element_type=F32
    )
    residual_keep[...] = (tokens.astype(F32) + projected).astype(BF16)
    residual = residual_keep[...].astype(F32)
    inv_rms = lax.rsqrt(jnp.mean(residual * residual, axis=-1, keepdims=True) + 1e-05)
    moe_in = (residual * inv_rms * gain_ref[...]).astype(BF16)
    either = (places[0] + places[1]).astype(BF16)
    exchange_build(0, jnp.dot(either, moe_in, preferred_element_type=F32).astype(BF16))
    exchange_start(0)
    for which in (0, 1, 2, 3):
        ring_sent(which)
    output_sent()
    load_start()
    for e in range(OWN):
        gather_4(1, e)
    exchange_end(0)
    gather_1(0, 0)
    gather_1(0, 1)
    gather_1(0, 2)
    gather_2(0, 0)
    gather_2(0, 1)
    gather_2(0, 2)
    gather_3(0, 0)
    gather_3(0, 1)
    gather_3(0, 2)
    for e in range(OWN):
        gather_5(1, e)
    gather_4(0, 0)
    gather_4(0, 1)
    gather_4(0, 2)
    gather_5(0, 0)
    compute(0)
    gather_5(0, 1)
    compute(1)
    reduce_2(0)
    gather_5(0, 2)
    compute(2)
    reduce_2(1)
    reduce_3(0)
    reduce_2(2)
    reduce_3(1)
    reduce_4(0)
    reduce_3(2)
    reduce_5(0)
    reduce_4(1)
    reduce_4(2)
    reduce_5(1)
    reduce_5(2)
    for copy in returned.values():
        copy.wait()
    for copy in reduces.values():
        copy.wait_send()
    for copy in stores[OWN - 1]:
        copy.wait()


def finish(ids, weights, back, residual, cot, gain, grads):
    vmem = pl.BlockSpec(memory_space=pltpu.VMEM)
    hbm = pl.BlockSpec(memory_space=pl.ANY)
    return pl.pallas_call(
        finish_kernel,
        out_shape=(
            jax.ShapeDtypeStruct((TOK, D), BF16),
            jax.ShapeDtypeStruct((TOK, D), BF16),
        )
        + tuple(jax.ShapeDtypeStruct(g.shape, BF16) for g in grads),
        in_specs=[vmem] * 6 + [hbm] * 3,
        out_specs=(vmem, vmem, hbm, hbm, hbm),
        scratch_shapes=[pltpu.VMEM(g.shape, BF16) for g in grads]
        + [pltpu.SemaphoreType.DMA((OWN, 3)), pltpu.SemaphoreType.DMA((OWN, 3))],
        compiler_params=pltpu.CompilerParams(vmem_limit_bytes=63 * 2**20),
        name="finish",
    )(ids, weights, back, residual, cot, gain, *grads)


def decoder_block(
    tokens, memory, bias, mem_session, session, cot, gain, ids, weights, projections, experts
):
    vmem = pl.BlockSpec(memory_space=pltpu.VMEM)
    hbm = pl.BlockSpec(memory_space=pl.ANY)
    corner = corner_matrix()
    dma = pltpu.SemaphoreType.DMA
    return pl.pallas_call(
        block_kernel,
        out_shape=(
            jax.ShapeDtypeStruct((N_SEQ, OWN * PACK, D), BF16),
            jax.ShapeDtypeStruct((TOK, D), BF16),
        )
        + tuple(jax.ShapeDtypeStruct(w.shape, BF16) for w in experts),
        in_specs=[vmem] * 12 + [hbm] * 7,
        out_specs=(vmem, vmem, hbm, hbm, hbm),
        scratch_shapes=[
            pltpu.VMEM((OWN, N_DP, BLK, D), BF16),
            pltpu.VMEM((OWN, D, 2 * HID), BF16),
            pltpu.VMEM((OWN + 1, HID, D), BF16),
            pltpu.VMEM((N_DP * SRC, HID), BF16),
            pltpu.VMEM((N_DP * SRC, 2 * HID), BF16),
            pltpu.VMEM((D, 2 * HID), BF16),
            pltpu.VMEM((MEM, D), BF16),
            pltpu.VMEM((N_SEQ, 8, MEM), F32),
            pltpu.VMEM((2, N_SEQ, 16, WIDE), BF16),
            pltpu.VMEM((2, N_SEQ, 16, WIDE), BF16),
            pltpu.VMEM((OWN, N_SEQ, PACK, D), BF16),
            pltpu.VMEM((OWN, 2, 4, BLK, HALF), BF16),
            pltpu.VMEM((OWN, 2, 2, 4, BLK, HALF), BF16),
            pltpu.VMEM((OWN, 2, 2, BLK, QUARTER), BF16),
            pltpu.VMEM((OWN, 2, 2, BLK, HALF), BF16),
            dma((5,)),
            dma((OWN, 3)),
            dma((OWN, 3)),
            dma((N_SEQ,)),
            dma((N_SEQ,)),
            dma((2, 3, 3)),
            dma((2, 3, 3)),
            dma((5, 8)),
            dma((5, 8)),
            dma((2, N_SEQ)),
            dma((2, N_SEQ)),
            dma((OWN, N_SEQ)),
            dma((OWN, N_SEQ)),
            dma((2, OWN, 2, 16)),
            dma((2, OWN, 2, 16)),
            dma((OWN, 2, 16)),
            dma((OWN, 2, 16)),
        ],
        compiler_params=pltpu.CompilerParams(
            collective_id=1, has_side_effects=True, vmem_limit_bytes=63 * 2**20
        ),
        name="decoder_block",
    )(
        tokens,
        bias,
        mem_session,
        session,
        cot,
        gain,
        ids,
        weights,
        jnp.asarray(compact_matrix(), BF16),
        jnp.asarray(corner, BF16),
        jnp.asarray(corner.T, BF16),
        jnp.asarray(return_matrix().T, BF16),
        memory,
        *projections,
        *experts,
    )


def per_device(
    tokens,
    memory,
    mem_session,
    dec_session,
    event_bias,
    expert_ids,
    route_weights,
    norm_gain,
    w_query,
    w_keyval,
    w_output,
    w_gate,
    w_up,
    w_down,
    cotangent,
):
    ids, weights = expert_ids[0].T, route_weights[0].T
    gain = norm_gain.reshape(1, D)
    back, residual, *grads = decoder_block(
        tokens[0],
        memory[0],
        event_bias[0],
        mem_session,
        dec_session,
        cotangent[0],
        gain,
        ids,
        weights,
        (w_query, w_keyval, w_output),
        (w_gate, w_up, w_down),
    )
    block_out, grad_resid, grad_gate, grad_up, grad_down = finish(
        ids, weights, back, residual, cotangent[0], gain, grads
    )
    return (block_out[None], grad_resid[None], grad_gate, grad_up, grad_down)


def solution(mesh):
    return jax.shard_map(
        per_device,
        mesh=mesh,
        in_specs=(
            P("dp", "seq", None),
            P("dp", "seq", None),
            P("dp", "seq"),
            P("dp", "seq"),
            P("dp", None, "seq"),
            P("dp", "seq", None),
            P("dp", "seq", None),
            P(),
            P("seq", None),
            P("seq", None),
            P("seq", None),
            P("seq", None, "dp"),
            P("seq", None, "dp"),
            P("seq", "dp", None),
            P("dp", "seq", None),
        ),
        out_specs=(
            P("dp", "seq", None),
            P("dp", "seq", None),
            P("seq", None, "dp"),
            P("seq", None, "dp"),
            P("seq", "dp", None),
        ),
        check_vma=False,
    )
```
